128 devices in a mesh: gx: 8 (over x, z_hi), gy: 16 (over z_lo, y, core).
Axes of the slice: x: 4, y: 4, z: 4 (z_hi: 2, z_lo: 2; z = z_hi * 2 + z_lo), core: 2. Of those that a mesh axis runs over, the one named last changes fastest.
Arguments:
- layer_input: bfloat16 [1024, 18432], P('gy', 'gx'), may hold values from -480 to 480
- ln_gain: float32 [18432], P('gx'), may hold values from 0.5 to 2
- w_query: bfloat16 [18432, 12288], P('gx', 'gy'), may hold values from -0.046875 to 0.046875
- w_keyval: bfloat16 [18432, 512], P('gx', 'gy'), may hold values from -0.046875 to 0.046875
- w_output: bfloat16 [12288, 18432], P('gy', 'gx'), may hold values from -0.4375 to 0.4375
- kv_cache: bfloat16 [1024, 2048, 512], P(('gx', 'gy')), may hold values from -150 to 150
- lengths: int32 [1024], P(('gx', 'gy')), may hold values from 1 to 2048, as said below
Outputs:
- attn_out: bfloat16 [1024, 18432], P('gy', 'gx')
The draws below stay inside these ranges and needn't reach their ends.
Inputs may be any that keep to these rules, and one draw needn't show every extreme that they name: `lengths`: slots at and beyond a row's length are ignored; some row has exactly 2048.
All inputs are finite; a program needn't handle non-finite values.
Results may differ from the reference program's by a relative error of at most 0.04.
Values may be sent and summed in bfloat16 or wider, within the bound.
A program may use at most 128 MiB of HBM per device.

```python
import math
import jax
import jax.numpy as jnp
from jax import lax

D = 18432
HQ = 48
HS = 256
CACHE = 2048
ROW_DEV = 8
BATCH = 1024
N_GY = 16


def draw_layer_input(key, part):
    key = jax.random.fold_in(key, 11)
    first, second, third = jax.random.split(key, 3)
    position = jnp.arange(D, dtype=jnp.float32) / D
    colscale = jnp.power(3.0, position) * jnp.exp(jax.random.uniform(second, (D,), jnp.float32, 0.0, math.log(4.0)))
    rowscale = jnp.exp(jax.random.uniform(third, (BATCH, 1), jnp.float32, 0.0, math.log(10.0)))
    base = jnp.clip(jax.random.normal(first, (BATCH, D), jnp.float32), -4.0, 4.0)
    return (base * colscale[None, :] * rowscale).astype(jnp.bfloat16)


def draw_kv_cache(key, part):
    key = jax.random.fold_in(key, 22)
    first = jax.random.fold_in(key, 0)
    base = jnp.clip(jax.random.normal(first, (BATCH, CACHE, 2 * HS), jnp.float32), -6.0, 6.0)
    return base.astype(jnp.bfloat16)


def draw_lengths(key, part):
    key = jax.random.fold_in(key, 33)
    first, second = jax.random.split(key, 2)
    drawn = jax.random.randint(first, (BATCH,), 1, CACHE + 1, jnp.int32)
    chosen = jax.random.randint(second, (), 0, BATCH, jnp.int32)
    return drawn.at[chosen].set(CACHE)


def shard_levels(key, extent, cuts, least, largest):
    loudness = 1.0
    for dim, parts in cuts:
        steps = jax.random.uniform(jax.random.fold_in(jax.random.fold_in(key, 6), dim), (parts,), jnp.float32, least / len(cuts), largest / len(cuts))
        loudness = loudness * jnp.repeat(jnp.exp(steps), extent[dim] // parts).reshape((-1,) + (1,) * (len(extent) - 1 - dim))
    return loudness


def centred(key, shape, spread, limit, shards=(), kind=jnp.bfloat16):
    result = spread * jax.random.normal(key, shape, jnp.float32)
    if shards:
        result = result * shard_levels(key, shape, shards, -0.22, 0.18)
    return jnp.clip(result, -limit, limit).astype(kind)


def setup_inputs(seed: int = 0) -> dict:
    streams_of = jax.random.split(jax.random.key(seed), 8)
    layer_input = draw_layer_input(jax.random.fold_in(streams_of[7], 71), 0)
    ln_gain = jnp.clip(jnp.exp(math.log(2.0) - 1.3862944 * jax.random.uniform(streams_of[1], (D,), jnp.float32) ** shard_levels(streams_of[1], (D,), ((0, 8),), -0.2, 0.2)), 0.5, 2.0)
    w_query = centred(streams_of[2], (D, HQ * HS), D ** -0.5, 0.046875, ((0, 8), (1, 16)))
    w_keyval = centred(streams_of[3], (D, 2 * HS), D ** -0.5, 0.046875, ((0, 8), (1, 16)))
    w_output = centred(streams_of[4], (HQ * HS, D), (HQ * HS // 64) ** -0.5, 0.4375, ((0, 16), (1, 8)))
    kv_cache = draw_kv_cache(jax.random.fold_in(streams_of[7], 71), 0)
    lengths = draw_lengths(jax.random.fold_in(streams_of[7], 71), 0)
    return {"layer_input": layer_input, "ln_gain": ln_gain, "w_query": w_query, "w_keyval": w_keyval, "w_output": w_output, "kv_cache": kv_cache, "lengths": lengths}


def attend(queries, new_kv, cache_rows, live_lengths):
    row_count = queries.shape[0]
    factor = HS ** (-0.5)
    query_heads = lax.optimization_barrier(queries).astype(jnp.float32).reshape(row_count, HQ, HS)
    fresh_kv = lax.optimization_barrier(new_kv).astype(jnp.float32)
    cached_keys = cache_rows[:, :, :HS].astype(jnp.float32)
    cached_values = cache_rows[:, :, HS:].astype(jnp.float32)
    scores = jnp.einsum('rhd,rcd->rhc', query_heads, cached_keys) * factor
    valid = lax.broadcasted_iota(jnp.int32, (row_count, 1, cache_rows.shape[1]), 2) < live_lengths[:, None, None]
    scores = jnp.where(valid, scores, jnp.float32(-1e+30))
    own_score = jnp.einsum('rhd,rd->rh', query_heads, fresh_kv[:, :HS]) * factor
    highest = jnp.maximum(lax.optimization_barrier(jnp.max(scores, axis=-1)), own_score)
    probs = jnp.exp(scores - highest[..., None])
    own_prob = jnp.exp(own_score - highest)
    denominator = lax.optimization_barrier(jnp.sum(probs, axis=-1)) + own_prob
    weights = lax.optimization_barrier((probs / denominator[..., None]).astype(jnp.bfloat16)).astype(jnp.float32)
    own_weight = lax.optimization_barrier((own_prob / denominator).astype(jnp.bfloat16)).astype(jnp.float32)
    mixed = jnp.einsum('rhc,rcd->rhd', weights, cached_values) + own_weight[..., None] * fresh_kv[:, None, HS:]
    return mixed.astype(jnp.bfloat16).reshape(row_count, HQ * HS)

def reference(layer_input, ln_gain, w_query, w_keyval, w_output, kv_cache, lengths):
    input_f32 = layer_input.astype(jnp.float32)
    average = lax.optimization_barrier(jnp.mean(input_f32, axis=1, keepdims=True))
    mean_square = lax.optimization_barrier(jnp.mean(input_f32 * input_f32, axis=1, keepdims=True))
    variance = mean_square - average * average
    normed = ((input_f32 - average) * lax.rsqrt(variance + 1e-05) * ln_gain[None, :]).astype(jnp.bfloat16)
    queries = jnp.dot(normed, w_query, preferred_element_type=jnp.float32).astype(jnp.bfloat16)
    keyval = jnp.dot(normed, w_keyval, preferred_element_type=jnp.float32).astype(jnp.bfloat16)
    groups = BATCH // ROW_DEV
    mixed = lax.map(lambda packed: attend(packed[0], packed[1], packed[2], packed[3]), (queries.reshape(groups, ROW_DEV, HQ * HS), keyval.reshape(groups, ROW_DEV, 2 * HS), kv_cache.reshape(groups, ROW_DEV, CACHE, 2 * HS), lengths.reshape(groups, ROW_DEV)))
    mixed = mixed.reshape(BATCH, HQ * HS)
    block_width = HQ * HS // N_GY
    blocks = jnp.transpose(mixed.reshape(BATCH, N_GY, block_width), (1, 0, 2))
    weight_blocks = w_output.reshape(N_GY, block_width, D)

    def add_block(carry, packed):
        partial_term = jnp.dot(packed[0], packed[1], preferred_element_type=jnp.float32).astype(jnp.bfloat16)
        return (carry + lax.optimization_barrier(partial_term).astype(jnp.float32), None)
    summed, _ = lax.scan(add_block, jnp.zeros((BATCH, D), jnp.float32), (blocks, weight_blocks))
    return summed.astype(jnp.bfloat16)
```

```python
import functools

import jax
import jax.numpy as jnp
from jax import lax
from jax.experimental import pallas as pl
from jax.experimental.pallas import tpu as pltpu
from jax.sharding import PartitionSpec as P

MESH = pl.DeviceIdType.MESH
F32 = jnp.float32
BF16 = jnp.bfloat16

HQ = 48
HS = 256
D = 18432
FEATURES = 2304
COLS = 768
KV = 32
CACHE = 2048
ROWS = 64
PAIR = 128
HALF = 400
OUT = 2304


class Ring:
    def __init__(self, device, pos, partner):
        self.device, self.pos, self.partner = device, pos, partner

    def near(self, step):
        return self.device(0, step)

    def across(self):
        return self.device(1, 0)


def gather_plan(ring, slot, ref, half, sends, recvs):
    def whole(i, dz, dr, target):
        place = slot(dz, dr)
        return pltpu.make_async_remote_copy(
            ref.at[place], ref.at[place], sends.at[i], recvs.at[i], device_id=target, device_id_type=MESH
        )

    def part(i, dz, dr, h, target):
        place = slot(dz, dr)
        piece = ref.at[place, pl.ds(h * half, half)]
        return pltpu.make_async_remote_copy(
            piece, piece, sends.at[i], recvs.at[i], device_id=target, device_id_type=MESH
        )

    up, down, across = ring.near(1), ring.near(-1), ring.across()
    outgoing = [
        lambda: whole(0, 0, 0, across),
        lambda: whole(1, 0, 0, up),
        lambda: whole(2, 0, 0, down),
        lambda: whole(3, 1, 0, up),
        lambda: whole(4, 1, 0, down),
        lambda: part(5, 0, -1, 0, up),
        lambda: part(6, 0, 1, 1, down),
        lambda: part(7, 1, -1, 0, up),
        lambda: part(8, 1, 1, 1, down),
    ]
    incoming = [
        lambda: whole(0, 1, 0, across),
        lambda: whole(1, 0, -1, up),
        lambda: whole(2, 0, 1, down),
        lambda: whole(3, 1, -1, up),
        lambda: whole(4, 1, 1, down),
        lambda: part(5, 0, 2, 0, up),
        lambda: part(6, 0, 2, 1, down),
        lambda: part(7, 1, 2, 0, up),
        lambda: part(8, 1, 2, 1, down),
    ]
    return outgoing, incoming


def arrival(s):
    dz = jnp.where((s == 1) | (s == 4) | (s == 5) | (s == 7), 1, 0)
    dr = jnp.where((s == 2) | (s == 4), 3, jnp.where((s == 3) | (s == 5), 1, jnp.where(s >= 6, 2, 0)))
    return dz, dr


class Reduce:
    def __init__(self, ring, mine, part, far, mid, zsend, zrecv, keep, sems):
        self.ring, self.mine, self.part, self.far, self.mid = ring, mine, part, far, mid
        self.zsend, self.zrecv, self.keep = zsend, zrecv, keep
        self.far_send, self.far_recv, self.mid_send, self.mid_recv, self.z_send, self.z_recv = sems

    def role(self, r):
        return lax.rem(r - self.ring.pos + 4, 4)

    def far_copy(self, k, h):
        target = self.ring.near(1 - 2 * h)
        return pltpu.make_async_remote_copy(
            self.part(k, h), self.far.at[k], self.far_send.at[k, h], self.far_recv.at[k],
            device_id=target, device_id_type=MESH,
        )

    def mid_copy(self, k, z, d, h, late):
        target = self.ring.near(1 - 2 * d)
        return pltpu.make_async_remote_copy(
            self.part(k, h), self.mid.at[z, d, h], self.mid_send.at[k, late], self.mid_recv.at[z, d, late],
            device_id=target, device_id_type=MESH,
        )

    def z_copy(self):
        return pltpu.make_async_remote_copy(
            self.zsend, self.zrecv, self.z_send, self.z_recv,
            device_id=self.ring.across(), device_id_type=MESH,
        )

    def first(self, k, z, r):
        role = self.role(r)

        @pl.when(role == 2)
        def _():
            self.far_copy(k, 0).start()
            self.far_copy(k, 1).start()

        @pl.when(lax.rem(role, 2) == 1)
        def _():
            d = role // 2
            self.mid_copy(k, z, d, 1 - d, 0).start()

    def second(self, k, z, r):
        role = self.role(r)

        @pl.when(lax.rem(role, 2) == 1)
        def _():
            d = role // 2
            self.far_copy(k, 0).wait_recv()
            piece = self.part(k, d)
            piece[...] = (piece[...].astype(F32) + self.far[k].astype(F32)).astype(BF16)
            self.mid_copy(k, z, d, d, 1).start()

    def third(self, k, z, r):
        role = self.role(r)

        @pl.when(role == 0)
        def _():
            for d in range(2):
                for late in range(2):
                    h = 1 - d if late == 0 else d
                    self.mid_copy(k, z, d, h, late).wait_recv()

            @pl.when(z != self.ring.partner)
            def _():
                for h in range(2):
                    total = self.part(k, h)[...].astype(F32)
                    total += self.mid[z, 0, h].astype(F32) + self.mid[z, 1, h].astype(F32)
                    self.zsend[h] = total.astype(BF16)
                self.z_copy().start()

            @pl.when(z == self.ring.partner)
            def _():
                for h in range(2):
                    total = self.part(k, h)[...].astype(F32)
                    total += self.mid[z, 0, h].astype(F32) + self.mid[z, 1, h].astype(F32)
                    self.keep[h] = total

    def finish(self, k, z, r):
        role = self.role(r)

        @pl.when(role == 2)
        def _():
            self.far_copy(k, 0).wait_send()
            self.far_copy(k, 1).wait_send()

        @pl.when(lax.rem(role, 2) == 1)
        def _():
            d = role // 2
            self.mid_copy(k, z, d, 1 - d, 0).wait_send()
            self.mid_copy(k, z, d, d, 1).wait_send()


def kernel(
    lengths, gain, x_hbm, wq_hbm, wkv_hbm, wo_hbm, kv_hbm, out_ref,
    x_own, xbuf, wq, wkv, wo, kv, stat_send, stats,
    part1, far1, mid1, zsend1, zrecv1, keep1,
    asend, arecv, qf, new_kv, osf, osend, orecv,
    abuf, tbuf, sib, far2, mid2, zsend2, zrecv2, keep2,
    load_sems, stat_ss, stat_rs, ag1_s, ag1_r, core1_s, core1_r,
    fs1, fr1, ms1, mr1, zs1, zr1, a_s, a_r, o_s, o_r, ag2_s, ag2_r,
    core2_s, core2_r, fs2, fr2, ms2, mr2, zs2, zr2,
):
    gx, gy = lax.axis_index("gx"), lax.axis_index("gy")
    x, zh = gx // 2, lax.rem(gx, 2)
    zl, y, c = gy // 8, lax.rem(gy // 2, 4), lax.rem(gy, 2)

    loads = [
        pltpu.make_async_copy(x_hbm, x_own, load_sems.at[0]),
        pltpu.make_async_copy(wq_hbm, wq, load_sems.at[1]),
        pltpu.make_async_copy(wkv_hbm, wkv, load_sems.at[2]),
        pltpu.make_async_copy(kv_hbm, kv, load_sems.at[3]),
        pltpu.make_async_copy(wo_hbm, wo, load_sems.at[4]),
    ]
    for load in loads:
        load.start()

    barrier = pltpu.get_barrier_semaphore()

    def greet_x(i, carry):
        pl.semaphore_signal(barrier, inc=1, device_id=(lax.rem(gx + i, 8), gy), device_id_type=MESH)
        return carry

    def greet_y(i, carry):
        pl.semaphore_signal(barrier, inc=1, device_id=(gx, lax.rem(gy + i, 16)), device_id_type=MESH)
        return carry

    lax.fori_loop(1, 8, greet_x, 0)
    lax.fori_loop(1, 16, greet_y, 0)

    def y_device(dz, dr):
        return (gx, (lax.rem(zl + dz, 2) * 4 + lax.rem(y + dr + 4, 4)) * 2 + c)

    def x_device(dz, dr):
        return (lax.rem(x + dr + 4, 4) * 2 + lax.rem(zh + dz, 2), gy)

    sibling = (gx, gy + 1 - 2 * c)
    y_ring = Ring(y_device, y, zl)
    x_ring = Ring(x_device, x, zh)

    loads[0].wait()
    row = x_own[...].astype(F32)
    sums = jnp.sum(row, axis=1, keepdims=True)
    squares = jnp.sum(row * row, axis=1, keepdims=True)
    lane = lax.broadcasted_iota(jnp.int32, (ROWS, 128), 1)
    tall = jnp.where(lane == 0, sums, jnp.where(lane == 1, squares, 0.0))
    stat_send[...] = jnp.concatenate([tall, tall], axis=0).T[0:8]
    stats[gx] = stat_send[...]

    pl.semaphore_wait(barrier, 22)

    def stat_copy(i):
        return pltpu.make_async_remote_copy(
            stat_send, stats.at[gx], stat_ss.at[i], stat_rs.at[i],
            device_id=(lax.rem(gx + i, 8), gy), device_id_type=MESH,
        )

    def stat_arrived(i):
        return pltpu.make_async_remote_copy(
            stat_send, stats.at[lax.rem(gx - i + 8, 8)], stat_ss.at[i], stat_rs.at[i],
            device_id=(lax.rem(gx + i, 8), gy), device_id_type=MESH,
        )

    def run(f):
        def body(i, carry):
            f(i)
            return carry

        return body

    lax.fori_loop(1, 8, run(lambda i: stat_copy(i).start()), 0)
    lax.fori_loop(1, 8, run(lambda i: stat_arrived(i).wait_recv()), 0)
    total = jnp.sum(stats[...], axis=0)
    wide = jnp.concatenate([total] * 16, axis=0).T
    average = wide[0:ROWS, 0:1] * (1.0 / D)
    variance = wide[0:ROWS, 1:2] * (1.0 / D) - average * average
    row = x_own[...].astype(F32)
    xbuf[gy] = ((row - average) * lax.rsqrt(variance + 1e-05) * gain[...]).astype(BF16)

    def y_slot(dz, dr):
        return y_device(dz, dr)[1]

    out1, in1 = gather_plan(y_ring, y_slot, xbuf, ROWS // 2, ag1_s, ag1_r)

    def core_copy1(i, dz, dr):
        place = y_slot(dz, dr)
        return pltpu.make_async_remote_copy(
            xbuf.at[place], xbuf.at[place], core1_s.at[i], core1_r.at[i], device_id=sibling, device_id_type=MESH
        )

    def core_arrived1(i, dz, dr):
        place = y_slot(dz, dr) + 1 - 2 * c
        return pltpu.make_async_remote_copy(
            xbuf.at[place], xbuf.at[place], core1_s.at[i], core1_r.at[i], device_id=sibling, device_id_type=MESH
        )

    reduce1 = Reduce(
        x_ring, None, lambda k, h: part1.at[k, h], far1, mid1, zsend1, zrecv1, keep1,
        (fs1, fr1, ms1, mr1, zs1.at[0], zr1.at[0]),
    )

    def chip1(s):
        dz, dr = arrival(s)
        k = lax.rem(zl + dz, 2) * 4 + lax.rem(y + dr, 4)
        return dz, dr, k, lax.rem(k, 2), k // 2

    def compute1(s):
        dz, dr, k, z, r = chip1(s)
        core_arrived1(s, dz, dr).wait_recv()
        lhs = xbuf[pl.ds(2 * k, 2)].reshape(PAIR, FEATURES)
        for t in range(3):
            q = jnp.dot(lhs, wq[:, t * 256 : (t + 1) * 256], preferred_element_type=F32).astype(BF16)
            for u in range(2):
                b = 2 * t + u
                part1[k, b // 3, pl.ds((b % 3) * 128, 128)] = q[:, u * 128 : (u + 1) * 128]
        new = jnp.dot(lhs, wkv[...], preferred_element_type=F32)
        packed = jnp.concatenate([new[32 * j : 32 * j + 32] for j in range(4)], axis=1).astype(BF16)
        part1[k, 0, pl.ds(384, 16)] = packed[0:16]
        part1[k, 1, pl.ds(384, 16)] = packed[16:32]
        reduce1.first(k, z, r)

    for i in range(3):
        out1[i]().start()
    core_copy1(0, 0, 0).start()
    loads[1].wait()
    loads[2].wait()

    def step1(s, carry):
        @pl.when(s == 1)
        def _():
            in1[0]().wait_recv()
            out1[3]().start()
            out1[4]().start()
            core_copy1(1, 1, 0).start()
            in1[1]().wait_recv()
            out1[5]().start()
            core_copy1(2, 0, -1).start()
            in1[2]().wait_recv()
            out1[6]().start()
            core_copy1(3, 0, 1).start()

        @pl.when(s == 4)
        def _():
            in1[3]().wait_recv()
            out1[7]().start()
            core_copy1(4, 1, -1).start()
            in1[4]().wait_recv()
            out1[8]().start()
            core_copy1(5, 1, 1).start()

        @pl.when(s == 6)
        def _():
            in1[5]().wait_recv()
            in1[6]().wait_recv()
            core_copy1(6, 0, 2).start()

        @pl.when(s == 7)
        def _():
            in1[7]().wait_recv()
            in1[8]().wait_recv()
            core_copy1(7, 1, 2).start()

        @pl.when(s < 8)
        def _():
            compute1(s)

        @pl.when((s >= 1) & (s < 9))
        def _():
            _, _, k, z, r = chip1(s - 1)
            reduce1.second(k, z, r)

        @pl.when(s >= 2)
        def _():
            _, _, k, z, r = chip1(s - 2)
            reduce1.third(k, z, r)

        return carry

    lax.fori_loop(0, 10, step1, 0)
    reduce1.z_copy().wait_recv()

    final = [keep1[h] + zrecv1[h].astype(F32) for h in range(2)]
    packed = jnp.concatenate([final[0][384:400], final[1][384:400]], axis=0).reshape(4, 8, 128)
    packed = jnp.concatenate([packed] * 4, axis=0)
    pieces = []
    for h in range(2):
        q = [final[h][b * 128 : (b + 1) * 128].reshape(16, 8, 128) for b in range(3)]
        pieces.append(jnp.concatenate(q + [packed], axis=2))
    asend[...] = jnp.concatenate(pieces, axis=1).astype(BF16)
    arecv[gy] = asend[gy]

    def all_to_all(src, dst, ss, rs):
        def copy(i):
            target = lax.rem(gy + i, 16)
            return pltpu.make_async_remote_copy(
                src.at[target], dst.at[gy], ss.at[i], rs.at[i], device_id=(gx, target), device_id_type=MESH
            )

        def arrived(i):
            target = lax.rem(gy + i, 16)
            return pltpu.make_async_remote_copy(
                src.at[target], dst.at[lax.rem(gy - i + 16, 16)], ss.at[i], rs.at[i],
                device_id=(gx, target), device_id_type=MESH,
            )

        lax.fori_loop(1, 16, run(lambda i: copy(i).start()), 0)
        lax.fori_loop(1, 16, run(lambda i: arrived(i).wait_recv()), 0)
        return copy

    a_copy = all_to_all(asend, arecv, a_s, a_r)

    got = arecv[...].astype(F32)
    for b in range(6):
        h, at = b // 3, (b % 3) * 128
        qf[b] = got[:, 8 * h : 8 * h + 8, at : at + 128].reshape(128, 128)
    fresh = got[:, 0:8, 384:512].reshape(128, 128)
    fresh = pltpu.roll(fresh, lax.rem(128 - 32 * (gy // 4), 128), 1)[:, 0:KV]
    for half in range(2):
        new_kv[:, half * HS : (half + 1) * HS] = jnp.concatenate(
            [fresh[8 * (8 * half + g) : 8 * (8 * half + g) + 8] for g in range(8)], axis=1
        )
    loads[3].wait()

    def attend(r, carry):
        lanes = [qf[b, pl.ds(r, 16, stride=8), :] for b in range(6)]
        q = jnp.concatenate([jnp.concatenate(lanes[2 * j : 2 * j + 2], axis=1) for j in range(3)], axis=0)
        fresh_row = new_kv[pl.ds(r, 1), :]
        scores = lax.dot_general(
            q.astype(BF16), kv[r, :, 0:HS], (((1,), (1,)), ((), ())), preferred_element_type=F32
        ) * (HS**-0.5)
        slot = lax.broadcasted_iota(jnp.int32, (HQ, CACHE), 1)
        scores = jnp.where(slot < lengths[r], scores, -1e30)
        own = jnp.sum(q * fresh_row[:, 0:HS], axis=1, keepdims=True) * (HS**-0.5)
        top = jnp.maximum(jnp.max(scores, axis=1, keepdims=True), own)
        probs = jnp.exp(scores - top)
        own_prob = jnp.exp(own - top)
        scale = 1.0 / (jnp.sum(probs, axis=1, keepdims=True) + own_prob)
        weights = (probs * scale).astype(BF16)
        own_weight = (own_prob * scale).astype(BF16).astype(F32)
        mixed = jnp.dot(weights, kv[r, :, HS : 2 * HS], preferred_element_type=F32)
        mixed += own_weight * fresh_row[:, HS : 2 * HS]
        for b in range(6):
            j, at = b // 2, (b % 2) * 128
            osf[b, pl.ds(r, 16, stride=8), :] = mixed[16 * j : 16 * j + 16, at : at + 128]
        return carry

    lax.fori_loop(0, 8, attend, 0)

    result = [jnp.concatenate([osf[3 * h + b].reshape(16, 8, 128) for b in range(3)], axis=2) for h in range(2)]
    osend[...] = jnp.concatenate(result, axis=1).astype(BF16)
    orecv[gy] = osend[gy]
    o_copy = all_to_all(osend, orecv, o_s, o_r)
    back = orecv[...].astype(F32)
    heads = jnp.concatenate([back[:, 0:8].reshape(PAIR, 384), back[:, 8:16].reshape(PAIR, 384)], axis=1)
    abuf[gx] = heads.astype(BF16)

    def x_slot(dz, dr):
        return x_device(dz, dr)[0]

    out2, in2 = gather_plan(x_ring, x_slot, abuf, PAIR // 2, ag2_s, ag2_r)
    reduce2 = Reduce(
        y_ring, None, lambda k, h: tbuf.at[k, c, pl.ds(h * 32, 32)], far2, mid2, zsend2, zrecv2, keep2,
        (fs2, fr2, ms2, mr2, zs2.at[0], zr2.at[0]),
    )

    def core_copy2(k):
        return pltpu.make_async_remote_copy(
            tbuf.at[k, 1 - c], sib.at[k], core2_s.at[k], core2_r.at[k], device_id=sibling, device_id_type=MESH
        )

    def chip2(s):
        dz, dr = arrival(s)
        k = lax.rem(x + dr, 4) * 2 + lax.rem(zh + dz, 2)
        return k, k // 4, lax.rem(k, 4)

    for i in range(3):
        out2[i]().start()
    loads[4].wait()

    def step2(s, carry):
        @pl.when(s == 1)
        def _():
            in2[0]().wait_recv()
            out2[3]().start()
            out2[4]().start()
            in2[1]().wait_recv()
            out2[5]().start()
            in2[2]().wait_recv()
            out2[6]().start()

        @pl.when(s == 4)
        def _():
            in2[3]().wait_recv()
            out2[7]().start()
            in2[4]().wait_recv()
            out2[8]().start()

        @pl.when(s == 6)
        def _():
            in2[5]().wait_recv()
            in2[6]().wait_recv()

        @pl.when(s == 7)
        def _():
            in2[7]().wait_recv()
            in2[8]().wait_recv()

        @pl.when(s < 8)
        def _():
            k, _, _ = chip2(s)
            lhs = abuf[k]
            for t in range(9):
                term = jnp.dot(lhs, wo[:, t * 256 : (t + 1) * 256], preferred_element_type=F32).astype(BF16)
                tbuf[k, 0, :, t * 256 : (t + 1) * 256] = term[0:ROWS]
                tbuf[k, 1, :, t * 256 : (t + 1) * 256] = term[ROWS:PAIR]
            core_copy2(k).start()

        @pl.when((s >= 1) & (s < 9))
        def _():
            k, z, r = chip2(s - 1)
            core_copy2(k).wait_recv()
            tbuf[k, c] = (tbuf[k, c].astype(F32) + sib[k].astype(F32)).astype(BF16)
            reduce2.first(k, z, r)

        @pl.when((s >= 2) & (s < 10))
        def _():
            k, z, r = chip2(s - 2)
            reduce2.second(k, z, r)

        @pl.when(s >= 3)
        def _():
            k, z, r = chip2(s - 3)
            reduce2.third(k, z, r)

        return carry

    lax.fori_loop(0, 11, step2, 0)
    reduce2.z_copy().wait_recv()
    for h in range(2):
        out_ref[pl.ds(h * 32, 32)] = (keep2[h] + zrecv2[h].astype(F32)).astype(BF16)

    lax.fori_loop(1, 8, run(lambda i: stat_copy(i).wait_send()), 0)
    lax.fori_loop(1, 16, run(lambda i: a_copy(i).wait_send()), 0)
    lax.fori_loop(1, 16, run(lambda i: o_copy(i).wait_send()), 0)
    for i in range(9):
        out1[i]().wait_send()
        out2[i]().wait_send()
    reduce1.z_copy().wait_send()
    reduce2.z_copy().wait_send()

    def drain(s, carry):
        dz, dr, k, z, r = chip1(s)
        core_copy1(s, dz, dr).wait_send()
        reduce1.finish(k, z, r)
        k, z, r = chip2(s)
        core_copy2(k).wait_send()
        reduce2.finish(k, z, r)
        return carry

    lax.fori_loop(0, 8, drain, 0)


def local(layer_input, ln_gain, w_query, w_keyval, w_output, kv_cache, lengths):
    any_space = pl.BlockSpec(memory_space=pl.ANY)
    vmem = pl.BlockSpec(memory_space=pltpu.VMEM)
    dma = pltpu.SemaphoreType.DMA
    scratch = [
        pltpu.VMEM((ROWS, FEATURES), BF16),
        pltpu.VMEM((16, ROWS, FEATURES), BF16),
        pltpu.VMEM((FEATURES, COLS), BF16),
        pltpu.VMEM((FEATURES, KV), BF16),
        pltpu.VMEM((COLS, OUT), BF16),
        pltpu.VMEM((8, CACHE, 2 * HS), BF16),
        pltpu.VMEM((8, 128), F32),
        pltpu.VMEM((8, 8, 128), F32),
        pltpu.VMEM((8, 2, HALF, 128), BF16),
        pltpu.VMEM((8, HALF, 128), BF16),
        pltpu.VMEM((2, 2, 2, HALF, 128), BF16),
        pltpu.VMEM((2, HALF, 128), BF16),
        pltpu.VMEM((2, HALF, 128), BF16),
        pltpu.VMEM((2, HALF, 128), F32),
        pltpu.VMEM((16, 16, 512), BF16),
        pltpu.VMEM((16, 16, 512), BF16),
        pltpu.VMEM((6, 128, 128), F32),
        pltpu.VMEM((8, 2 * HS), F32),
        pltpu.VMEM((6, 128, 128), F32),
        pltpu.VMEM((16, 16, 384), BF16),
        pltpu.VMEM((16, 16, 384), BF16),
        pltpu.VMEM((8, PAIR, COLS), BF16),
        pltpu.VMEM((8, 2, ROWS, OUT), BF16),
        pltpu.VMEM((8, ROWS, OUT), BF16),
        pltpu.VMEM((8, ROWS // 2, OUT), BF16),
        pltpu.VMEM((2, 2, 2, ROWS // 2, OUT), BF16),
        pltpu.VMEM((2, ROWS // 2, OUT), BF16),
        pltpu.VMEM((2, ROWS // 2, OUT), BF16),
        pltpu.VMEM((2, ROWS // 2, OUT), F32),
        dma((5,)),
        dma((8,)), dma((8,)),
        dma((9,)), dma((9,)),
        dma((8,)), dma((8,)),
        dma((8, 2)), dma((8,)), dma((8, 2)), dma((2, 2, 2)), dma((1,)), dma((1,)),
        dma((16,)), dma((16,)), dma((16,)), dma((16,)),
        dma((9,)), dma((9,)),
        dma((8,)), dma((8,)),
        dma((8, 2)), dma((8,)), dma((8, 2)), dma((2, 2, 2)), dma((1,)), dma((1,)),
    ]
    return pl.pallas_call(
        kernel,
        name="decode_attention",
        out_shape=jax.ShapeDtypeStruct((ROWS, OUT), BF16),
        in_specs=[pl.BlockSpec(memory_space=pltpu.SMEM), vmem] + [any_space] * 5,
        out_specs=vmem,
        scratch_shapes=scratch,
        compiler_params=pltpu.CompilerParams(
            collective_id=0, has_side_effects=True, vmem_limit_bytes=60 << 20
        ),
        cost_estimate=pl.CostEstimate(flops=8_300_000_000, bytes_accessed=25_000_000, transcendentals=800_000),
    )(lengths, ln_gain.reshape(1, FEATURES), layer_input, w_query, w_keyval, w_output, kv_cache)


def solution(mesh):
    in_specs = (
        P("gy", "gx"),
        P("gx"),
        P("gx", "gy"),
        P("gx", "gy"),
        P("gy", "gx"),
        P(("gx", "gy"), None, None),
        P(("gx", "gy")),
    )
    out_specs = P("gy", "gx")
    return jax.shard_map(local, mesh=mesh, in_specs=in_specs, out_specs=out_specs, check_vma=False)
```

```python
import functools

import jax
import jax.numpy as jnp
from jax import lax
from jax.experimental import pallas as pl
from jax.experimental.pallas import tpu as pltpu
from jax.sharding import PartitionSpec as P

MESH = pl.DeviceIdType.MESH
F32 = jnp.float32
BF16 = jnp.bfloat16

HQ = 48
HS = 256
D = 18432
FEATURES = 2304
COLS = 768
KV = 32
CACHE = 2048
ROWS = 64
PAIR = 128
HALF = 400
LAST = 144
OUT = 2304


FAR_FIRST = (12, 4, 11, 13, 5, 3, 10, 14, 6, 2, 8, 9, 7, 15, 1)


class Ring:
    def __init__(self, device, pos, partner):
        self.device, self.pos, self.partner = device, pos, partner

    def near(self, step):
        return self.device(0, step)

    def across(self):
        return self.device(1, 0)


def taken(ref, sem):
    pltpu.make_async_copy(ref, ref, sem).wait()


def gather_plan(ring, slot, ref, half, send, recvs):
    def whole(i, dz, dr, target):
        place = slot(dz, dr)
        return pltpu.make_async_remote_copy(
            ref.at[place], ref.at[place], send, recvs.at[i], device_id=target, device_id_type=MESH
        )

    def part(i, dz, dr, h, target):
        place = slot(dz, dr)
        piece = ref.at[place, pl.ds(h * half, half)]
        return pltpu.make_async_remote_copy(
            piece, piece, send, recvs.at[i], device_id=target, device_id_type=MESH
        )

    up, down, across = ring.near(1), ring.near(-1), ring.across()
    outgoing = [
        lambda: part(0, 0, 0, 0, across),
        lambda: part(1, 0, 0, 1, across),
        lambda: whole(2, 0, 0, up),
        lambda: whole(3, 0, 0, down),
        lambda: part(4, 1, 0, 0, up),
        lambda: part(5, 1, 0, 0, down),
        lambda: part(6, 1, 0, 1, up),
        lambda: part(7, 1, 0, 1, down),
        lambda: part(8, 0, -1, 0, up),
        lambda: part(9, 0, 1, 1, down),
        lambda: part(10, 1, -1, 0, up),
        lambda: part(11, 1, 1, 1, down),
    ]
    incoming = [
        lambda: part(0, 1, 0, 0, across),
        lambda: part(1, 1, 0, 1, across),
        lambda: whole(2, 0, -1, up),
        lambda: whole(3, 0, 1, down),
        lambda: part(4, 1, -1, 0, up),
        lambda: part(5, 1, 1, 0, down),
        lambda: part(6, 1, -1, 1, up),
        lambda: part(7, 1, 1, 1, down),
        lambda: part(8, 0, 2, 0, up),
        lambda: part(9, 0, 2, 1, down),
        lambda: part(10, 1, 2, 0, up),
        lambda: part(11, 1, 2, 1, down),
    ]
    return outgoing, incoming


def arrival(s):
    dz = jnp.where((s == 1) | (s == 4) | (s == 5) | (s == 7), 1, 0)
    dr = jnp.where((s == 2) | (s == 4), 3, jnp.where((s == 3) | (s == 5), 1, jnp.where(s >= 6, 2, 0)))
    return dz, dr


class Reduce:
    def __init__(self, ring, part, far, mid, zsend, zrecv, keep, sems):
        self.ring, self.part, self.far, self.mid = ring, part, far, mid
        self.zsend, self.zrecv, self.keep = zsend, zrecv, keep
        self.send, self.far_recv, self.mid_recv, self.z_send, self.z_recv = sems

    def role(self, r):
        return lax.rem(r - self.ring.pos + 4, 4)

    def far_copy(self, k, z, p, h):
        target = self.ring.near(1 - 2 * h)
        return pltpu.make_async_remote_copy(
            self.part(k, p, h), self.far(z, h, p), self.send, self.far_recv.at[z, h, p],
            device_id=target, device_id_type=MESH,
        )

    def mid_copy(self, k, z, p, d, h):
        target = self.ring.near(1 - 2 * d)
        return pltpu.make_async_remote_copy(
            self.part(k, p, h), self.mid(z, d, p, h), self.send, self.mid_recv.at[z, d, p],
            device_id=target, device_id_type=MESH,
        )

    def z_copy(self, p, h):
        return pltpu.make_async_remote_copy(
            self.zsend(p, h), self.zrecv(p, h), self.z_send, self.z_recv.at[p],
            device_id=self.ring.across(), device_id_type=MESH,
        )

    def first(self, k, z, r, p):
        role = self.role(r)

        @pl.when(role == 2)
        def _():
            self.far_copy(k, z, p, 0).start()
            self.far_copy(k, z, p, 1).start()

        @pl.when(lax.rem(role, 2) == 1)
        def _():
            d = role // 2
            self.mid_copy(k, z, p, d, 1 - d).start()

    def second(self, k, z, r):
        role = self.role(r)

        @pl.when(lax.rem(role, 2) == 1)
        def _():
            d = role // 2
            for p in range(3):
                self.far_copy(k, z, p, d).wait_recv()
                piece = self.part(k, p, d)
                piece[...] = (piece[...].astype(F32) + self.far(z, d, p)[...].astype(F32)).astype(BF16)
                self.mid_copy(k, z, p, d, d).start()

    def third(self, k, z, r):
        role = self.role(r)

        def total(p, h):
            sums = self.mid(z, 0, p, h)[...].astype(F32) + self.mid(z, 1, p, h)[...].astype(F32)
            return self.part(k, p, h)[...].astype(F32) + sums

        @pl.when(role == 0)
        def _():
            for p in range(3):
                for d in range(2):
                    taken(self.mid(z, d, p, None), self.mid_recv.at[z, d, p])

                @pl.when(z != self.ring.partner)
                def _():
                    for h in range(2):
                        self.zsend(p, h)[...] = total(p, h).astype(BF16)
                        self.z_copy(p, h).start()

                @pl.when(z == self.ring.partner)
                def _():
                    for h in range(2):
                        self.keep(p, h)[...] = total(p, h)

    def result(self, p):
        taken(self.zrecv(p, None), self.z_recv.at[p])
        return [self.keep(p, h)[...] + self.zrecv(p, h)[...].astype(F32) for h in range(2)]

    def finish(self, six_blocks, one_block):
        taken(six_blocks, self.send)
        taken(one_block, self.z_send)


def run(f):
    def body(i, carry):
        f(i)
        return carry

    return body


def loop(start, stop, f):
    lax.fori_loop(start, stop, run(f), 0)


def to_columns(rows):
    return jnp.concatenate([rows] * 16, axis=0).T


def kernel(
    lengths_hbm, gain_hbm, x_hbm, wq_hbm, wkv_hbm, wo_hbm, kv_hbm, out_hbm,
    lengths, gain, out,
    xbuf, lhs, wq, wkv, wo, kv, stat_send, stats, row_stats,
    part1, far1, mid1, zsend1, zrecv1, keep1,
    asend, arecv, qf, new_kv, scores, osf, osend, orecv,
    abuf, tbuf, sib, far2, mid2, zsend2, zrecv2, keep2,
    load_sems, out_sems, stat_s, stat_r, row_s, row_r, ag1_s, ag1_r, core1_s, core1_r,
    send1, far1_r, mid1_r, z1_s, z1_r, a_s, a_r, o_s, o_r, ag2_s, ag2_r, core2_s, core2_r,
    send2, far2_r, mid2_r, z2_s, z2_r,
):
    gx, gy = lax.axis_index("gx"), lax.axis_index("gy")
    x, zh = gx // 2, lax.rem(gx, 2)
    zl, y, c = gy // 8, lax.rem(gy // 2, 4), lax.rem(gy, 2)

    loads = [
        pltpu.make_async_copy(x_hbm, xbuf.at[gy], load_sems.at[0]),
        pltpu.make_async_copy(wq_hbm, wq, load_sems.at[1]),
        pltpu.make_async_copy(wkv_hbm, wkv, load_sems.at[2]),
        pltpu.make_async_copy(kv_hbm, kv, load_sems.at[3]),
        pltpu.make_async_copy(wo_hbm, wo, load_sems.at[4]),
        pltpu.make_async_copy(gain_hbm, gain, load_sems.at[5]),
        pltpu.make_async_copy(lengths_hbm, lengths, load_sems.at[6]),
    ]
    loads[0].start()

    barrier = pltpu.get_barrier_semaphore()

    def greet(target):
        pl.semaphore_signal(barrier, inc=1, device_id=target, device_id_type=MESH)

    loop(1, 8, lambda i: greet((lax.rem(gx + i, 8), gy)))
    loop(1, 16, lambda i: greet((gx, lax.rem(gy + i, 16))))

    def y_device(dz, dr):
        return (gx, (lax.rem(zl + dz, 2) * 4 + lax.rem(y + dr + 4, 4)) * 2 + c)

    def x_device(dz, dr):
        return (lax.rem(x + dr + 4, 4) * 2 + lax.rem(zh + dz, 2), gy)

    sibling = (gx, gy + 1 - 2 * c)
    y_ring = Ring(y_device, y, zl)
    x_ring = Ring(x_device, x, zh)

    loads[0].wait()
    for load in loads[1:]:
        load.start()
    row = xbuf[gy].astype(F32)
    sums = jnp.sum(row, axis=1, keepdims=True)
    squares = jnp.sum(row * row, axis=1, keepdims=True)
    lane = lax.broadcasted_iota(jnp.int32, (ROWS, 128), 1)
    tall = jnp.where(lane == 0, sums, jnp.where(lane == 1, squares, 0.0))
    stat_send[...] = jnp.concatenate([tall, tall], axis=0).T[0:8]
    stats[gx] = stat_send[...]

    pl.semaphore_wait(barrier, 22)

    def y_slot(dz, dr):
        return y_device(dz, dr)[1]

    out1, in1 = gather_plan(y_ring, y_slot, xbuf, ROWS // 2, ag1_s.at[0], ag1_r)

    def core_copy1(i, dz, dr):
        place = y_slot(dz, dr)
        return pltpu.make_async_remote_copy(
            xbuf.at[place], xbuf.at[place], core1_s.at[0], core1_r.at[i], device_id=sibling, device_id_type=MESH
        )

    def core_arrived1(i, dz, dr):
        place = y_slot(dz, dr) + 1 - 2 * c
        return pltpu.make_async_remote_copy(
            xbuf.at[place], xbuf.at[place], core1_s.at[0], core1_r.at[i], device_id=sibling, device_id_type=MESH
        )

    def stat_copy(i, slot):
        return pltpu.make_async_remote_copy(
            stat_send, stats.at[slot], stat_s.at[0], stat_r.at[0],
            device_id=(lax.rem(gx + i, 8), gy), device_id_type=MESH,
        )

    def row_copy(i, slot):
        return pltpu.make_async_remote_copy(
            row_stats.at[slot], row_stats.at[slot], row_s.at[0], row_r.at[i],
            device_id=(gx, lax.rem(gy + i, 16)), device_id_type=MESH,
        )

    loop(1, 8, lambda i: stat_copy(i, gx).start())
    for i in range(4):
        out1[i]().start()
    core_copy1(0, 0, 0).start()

    taken(stats.at[pl.ds(0, 7)], stat_r.at[0])
    total = jnp.sum(stats[...], axis=0)
    average = total[0:1] * (1.0 / D)
    variance = total[1:2] * (1.0 / D) - average * average
    deviation = lax.rsqrt(variance + 1e-05)
    row_stats[gy] = jnp.concatenate([average, deviation, jnp.zeros((6, 128), F32)], axis=0)
    for i in FAR_FIRST:
        row_copy(i, gy).start()

    def rows1(p):
        return pl.ds(128 * p, LAST if p == 2 else 128)

    def both(h):
        return pl.ds(0, 2) if h is None else h

    reduce1 = Reduce(
        x_ring,
        lambda k, p, h: part1.at[k, h, rows1(p)],
        lambda z, d, p: far1.at[z, d, rows1(p)],
        lambda z, d, p, h: mid1.at[z, d, both(h), rows1(p)],
        lambda p, h: zsend1.at[h, rows1(p)],
        lambda p, h: zrecv1.at[both(h), rows1(p)],
        lambda p, h: keep1.at[h, rows1(p)],
        (send1.at[0], far1_r, mid1_r, z1_s.at[0], z1_r),
    )

    def chip1(s):
        dz, dr = arrival(s)
        k = lax.rem(zl + dz, 2) * 4 + lax.rem(y + dr, 4)
        return k, lax.rem(k, 2), k // 2

    def compute1(s):
        k, z, r = chip1(s)
        dz, dr = arrival(s)
        for u in range(2):
            source = 2 * k + u
            i = lax.rem(gy - source + 16, 16)

            @pl.when(i > 0)
            def _():
                row_copy(i, source).wait_recv()

        core_arrived1(s, dz, dr).wait_recv()
        first_lanes = lax.broadcasted_iota(jnp.int32, (8, 128), 1) < ROWS
        columns = to_columns(jnp.where(first_lanes, row_stats[2 * k], row_stats[2 * k + 1]))
        rows = xbuf[pl.ds(2 * k, 2)].reshape(PAIR, FEATURES).astype(F32)
        lhs[...] = ((rows - columns[:, 0:1]) * columns[:, 1:2] * gain[...].reshape(1, FEATURES)).astype(BF16)
        for p in range(3):
            q = jnp.dot(lhs[...], wq[:, p * 256 : (p + 1) * 256], preferred_element_type=F32).astype(BF16)
            for h in range(2):
                part1[k, h, pl.ds(128 * p, 128)] = q[:, h * 128 : (h + 1) * 128]
            if p == 2:
                new = lax.dot_general(
                    wkv[...], lhs[...], (((1,), (1,)), ((), ())), preferred_element_type=F32
                ).astype(BF16)
                for h in range(2):
                    part1[k, h, pl.ds(384, 16)] = new[16 * h : 16 * h + 16]
            reduce1.first(k, z, r, p)

    in1[0]().wait_recv()
    out1[4]().start()
    out1[5]().start()
    in1[1]().wait_recv()
    out1[6]().start()
    out1[7]().start()
    core_copy1(1, 1, 0).start()
    in1[2]().wait_recv()
    out1[8]().start()
    core_copy1(2, 0, -1).start()
    in1[3]().wait_recv()
    out1[9]().start()
    core_copy1(3, 0, 1).start()
    loads[1].wait()
    loads[2].wait()
    loads[5].wait()

    def second1(s):
        reduce1.second(*chip1(s))

    def third1(s):
        reduce1.third(*chip1(s))

    def step1(s):
        @pl.when(s == 4)
        def _():
            loop(0, 2, second1)
            in1[4]().wait_recv()
            out1[10]().start()
            in1[7]().wait_recv()
            out1[11]().start()
            in1[6]().wait_recv()
            core_copy1(4, 1, -1).start()
            in1[5]().wait_recv()
            core_copy1(5, 1, 1).start()

        @pl.when(s == 6)
        def _():
            loop(2, 4, second1)
            in1[8]().wait_recv()
            in1[9]().wait_recv()
            core_copy1(6, 0, 2).start()
            loop(0, 2, third1)

        @pl.when(s == 7)
        def _():
            loop(2, 4, third1)
            in1[10]().wait_recv()
            in1[11]().wait_recv()
            core_copy1(7, 1, 2).start()
            loop(4, 6, second1)

        compute1(s)

    loop(0, 8, step1)
    loop(6, 8, second1)
    loop(4, 8, third1)

    final = [reduce1.result(p) for p in range(3)]
    blocks = [final[p][h][0:128].reshape(16, 8, 128) for p in range(3) for h in range(2)]
    fresh = jnp.concatenate([final[2][0][128:144], final[2][1][128:144]] * 4, axis=0).T.reshape(16, 8, 128)
    halves = [jnp.concatenate(blocks[3 * h : 3 * h + 3] + [fresh], axis=2) for h in range(2)]
    asend[...] = jnp.concatenate(halves, axis=1).astype(BF16)
    arecv[gy] = asend[gy]

    def all_to_all(src, dst, ss, rs):
        for i in FAR_FIRST:
            target = lax.rem(gy + i, 16)
            pltpu.make_async_remote_copy(
                src.at[target], dst.at[gy], ss, rs, device_id=(gx, target), device_id_type=MESH
            ).start()
        taken(dst.at[pl.ds(0, 15)], rs)

    all_to_all(asend, arecv, a_s.at[0], a_r.at[0])

    got = arecv[...].astype(F32)
    for b in range(6):
        h, at = b // 3, (b % 3) * 128
        qf[b] = got[:, 8 * h : 8 * h + 8, at : at + 128].reshape(128, 128)
    fresh = got[:, 0:8, 384 : 384 + KV]
    for half in range(2):
        new_kv[:, half * HS : (half + 1) * HS] = jnp.concatenate([fresh[8 * half + g] for g in range(8)], axis=1)
    loads[3].wait()
    loads[6].wait()

    def query(r):
        lanes = [qf[b, pl.ds(r, 16, stride=8), :] for b in range(6)]
        return jnp.concatenate([jnp.concatenate(lanes[2 * j : 2 * j + 2], axis=1) for j in range(3)], axis=0)

    for r in range(8):
        scores[r] = lax.dot_general(
            (query(r) * (HS**-0.5)).astype(BF16), kv[r, :, 0:HS], (((1,), (1,)), ((), ())),
            preferred_element_type=F32,
        )
    slot = lax.broadcasted_iota(jnp.int32, (1, CACHE), 1)
    for r in range(8):
        fresh_row = new_kv[r : r + 1, :]
        score = scores[r] + jnp.where(slot < lengths[r], 0.0, -1e30)
        own = jnp.sum(query(r) * fresh_row[:, 0:HS], axis=1, keepdims=True) * (HS**-0.5)
        top = jnp.maximum(jnp.max(score, axis=1, keepdims=True), own)
        probs = jnp.exp(score - top)
        own_prob = jnp.exp(own - top)
        scale = 1.0 / (jnp.sum(probs, axis=1, keepdims=True) + own_prob)
        mixed = jnp.dot(probs.astype(BF16), kv[r, :, HS : 2 * HS], preferred_element_type=F32)
        mixed = (mixed + own_prob * fresh_row[:, HS : 2 * HS]) * scale
        for b in range(6):
            j, at = b // 2, (b % 2) * 128
            osf[b, pl.ds(r, 16, stride=8), :] = mixed[16 * j : 16 * j + 16, at : at + 128]

    result = [jnp.concatenate([osf[3 * h + b].reshape(16, 8, 128) for b in range(3)], axis=2) for h in range(2)]
    osend[...] = jnp.concatenate(result, axis=1).astype(BF16)
    orecv[gy] = osend[gy]
    all_to_all(osend, orecv, o_s.at[0], o_r.at[0])
    back = orecv[...].astype(F32)
    heads = jnp.concatenate([back[:, 0:8].reshape(PAIR, 384), back[:, 8:16].reshape(PAIR, 384)], axis=1)
    abuf[gx] = heads.astype(BF16)

    def x_slot(dz, dr):
        return x_device(dz, dr)[0]

    out2, in2 = gather_plan(x_ring, x_slot, abuf, PAIR // 2, ag2_s.at[0], ag2_r)
    reduce2 = Reduce(
        y_ring,
        lambda k, p, h: tbuf.at[k, p, c, pl.ds(h * 32, 32)],
        lambda z, d, p: far2.at[z, d, p],
        lambda z, d, p, h: mid2.at[z, d, p, both(h)],
        lambda p, h: zsend2.at[p, h],
        lambda p, h: zrecv2.at[p, both(h)],
        lambda p, h: keep2.at[p, h],
        (send2.at[0], far2_r, mid2_r, z2_s.at[0], z2_r),
    )

    def core_copy2(k, p):
        return pltpu.make_async_remote_copy(
            tbuf.at[k, p, 1 - c], sib.at[k, p], core2_s.at[0], core2_r.at[k, p],
            device_id=sibling, device_id_type=MESH,
        )

    same = jnp.where(x // 2 == zl, 1, 0)
    twin = jnp.where(lax.rem(x, 2) == 0, 1, 3)

    def chip2(s):
        near = jnp.where((s == 3) | (s == 7), twin, 4 - twin)
        dr_same = jnp.where(s < 2, 0, jnp.where((s == 5) | (s == 6), 2, near))
        dz_same = jnp.where((s == 1) | (s == 4) | (s >= 6), 1, 0)
        near = jnp.where((s == 2) | (s == 4), twin, 4 - twin)
        dr_else = jnp.where(s < 2, 0, jnp.where(s >= 6, 2, near))
        dz_else = jnp.where((s == 1) | (s == 4) | (s == 5) | (s == 7), 1, 0)
        dr = same * dr_same + (1 - same) * dr_else
        dz = same * dz_same + (1 - same) * dz_else
        k = lax.rem(x + dr, 4) * 2 + lax.rem(zh + dz, 2)
        return k, k // 4, lax.rem(k, 4)

    for i in range(4):
        out2[i]().start()
    loads[4].wait()

    def first2(s):
        k, z, r = chip2(s)
        for p in range(3):
            core_copy2(k, p).wait_recv()
            tbuf[k, p, c] = (tbuf[k, p, c].astype(F32) + sib[k, p].astype(F32)).astype(BF16)
            reduce2.first(k, z, r, p)

    def second2(s):
        reduce2.second(*chip2(s))

    def third2(s):
        reduce2.third(*chip2(s))

    def step2(s):
        @pl.when(s == 1)
        def _():
            first2(0)
            in2[0]().wait_recv()
            out2[4]().start()
            out2[5]().start()
            in2[1]().wait_recv()
            out2[6]().start()
            out2[7]().start()
            in2[2]().wait_recv()
            out2[8]().start()
            in2[3]().wait_recv()
            out2[9]().start()

        @pl.when(s == 4)
        def _():
            first2(3)
            second2(0)
            in2[4]().wait_recv()
            out2[10]().start()
            in2[7]().wait_recv()
            out2[11]().start()
            in2[6]().wait_recv()
            in2[5]().wait_recv()

        @pl.when(s == 6 - same)
        def _():
            in2[8]().wait_recv()
            in2[9]().wait_recv()

        @pl.when(s == 7 - same)
        def _():
            in2[10]().wait_recv()
            in2[11]().wait_recv()

        k, _, _ = chip2(s)
        rows = abuf[k]
        for p in range(3):
            for t in range(3):
                at = (3 * p + t) * 256
                term = jnp.dot(rows, wo[:, at : at + 256], preferred_element_type=F32).astype(BF16)
                tbuf[k, p, 0, :, t * 256 : (t + 1) * 256] = term[0:ROWS]
                tbuf[k, p, 1, :, t * 256 : (t + 1) * 256] = term[ROWS:PAIR]
            core_copy2(k, p).start()

        @pl.when((s > 1) & (s != 4))
        def _():
            first2(s - 1)

        @pl.when(s >= 4)
        def _():
            second2(s - 3)

        @pl.when(s == 7)
        def _():
            loop(0, 2, third2)

    loop(0, 8, step2)
    first2(7)
    loop(5, 8, second2)
    loop(2, 8, third2)
    writes = []
    for p in range(3):
        for h, rows in enumerate(reduce2.result(p)):
            out[pl.ds(h * 32, 32), p * 768 : (p + 1) * 768] = rows.astype(BF16)
        columns = pl.ds(p * 768, 768)
        writes.append(pltpu.make_async_copy(out.at[:, columns], out_hbm.at[:, columns], out_sems.at[p]))
        writes[p].start()

    taken(stats.at[pl.ds(0, 7)], stat_s.at[0])
    taken(row_stats.at[pl.ds(0, 15)], row_s.at[0])
    taken(asend.at[pl.ds(0, 15)], a_s.at[0])
    taken(osend.at[pl.ds(0, 15)], o_s.at[0])
    taken(xbuf.at[pl.ds(0, 7)], ag1_s.at[0])
    taken(abuf.at[pl.ds(0, 7)], ag2_s.at[0])
    taken(xbuf.at[pl.ds(0, 8)], core1_s.at[0])
    taken(sib, core2_s.at[0])
    reduce1.finish(part1.at[pl.ds(0, 6)], zsend1)
    reduce2.finish(tbuf.at[pl.ds(0, 6), :, 0], zsend2)
    for write in writes:
        write.wait()


def local(layer_input, ln_gain, w_query, w_keyval, w_output, kv_cache, lengths):
    any_space = pl.BlockSpec(memory_space=pl.ANY)
    dma = pltpu.SemaphoreType.DMA
    scratch = [
        pltpu.SMEM((8,), jnp.int32),
        pltpu.VMEM((FEATURES,), F32),
        pltpu.VMEM((ROWS, OUT), BF16),
        pltpu.VMEM((16, ROWS, FEATURES), BF16),
        pltpu.VMEM((PAIR, FEATURES), BF16),
        pltpu.VMEM((FEATURES, COLS), BF16),
        pltpu.VMEM((KV, FEATURES), BF16),
        pltpu.VMEM((COLS, OUT), BF16),
        pltpu.VMEM((8, CACHE, 2 * HS), BF16),
        pltpu.VMEM((8, 128), F32),
        pltpu.VMEM((8, 8, 128), F32),
        pltpu.VMEM((16, 8, 128), F32),
        pltpu.VMEM((8, 2, HALF, 128), BF16),
        pltpu.VMEM((2, 2, HALF, 128), BF16),
        pltpu.VMEM((2, 2, 2, HALF, 128), BF16),
        pltpu.VMEM((2, HALF, 128), BF16),
        pltpu.VMEM((2, HALF, 128), BF16),
        pltpu.VMEM((2, HALF, 128), F32),
        pltpu.VMEM((16, 16, 512), BF16),
        pltpu.VMEM((16, 16, 512), BF16),
        pltpu.VMEM((6, 128, 128), F32),
        pltpu.VMEM((8, 2 * HS), F32),
        pltpu.VMEM((8, HQ, CACHE), F32),
        pltpu.VMEM((6, 128, 128), F32),
        pltpu.VMEM((16, 16, 384), BF16),
        pltpu.VMEM((16, 16, 384), BF16),
        pltpu.VMEM((8, PAIR, COLS), BF16),
        pltpu.VMEM((8, 3, 2, ROWS, 768), BF16),
        pltpu.VMEM((8, 3, ROWS, 768), BF16),
        pltpu.VMEM((2, 2, 3, 32, 768), BF16),
        pltpu.VMEM((2, 2, 3, 2, 32, 768), BF16),
        pltpu.VMEM((3, 2, 32, 768), BF16),
        pltpu.VMEM((3, 2, 32, 768), BF16),
        pltpu.VMEM((3, 2, 32, 768), F32),
        dma((7,)), dma((3,)),
        dma((1,)), dma((1,)), dma((1,)), dma((16,)),
        dma((1,)), dma((12,)), dma((1,)), dma((8,)),
        dma((1,)), dma((2, 2, 3)), dma((2, 2, 3)), dma((1,)), dma((3,)),
        dma((1,)), dma((1,)), dma((1,)), dma((1,)),
        dma((1,)), dma((12,)), dma((1,)), dma((8, 3)),
        dma((1,)), dma((2, 2, 3)), dma((2, 2, 3)), dma((1,)), dma((3,)),
    ]
    return pl.pallas_call(
        kernel,
        name="decode_attention",
        out_shape=jax.ShapeDtypeStruct((ROWS, OUT), BF16),
        in_specs=[any_space] * 7,
        out_specs=any_space,
        scratch_shapes=scratch,
        compiler_params=pltpu.CompilerParams(
            collective_id=0, has_side_effects=True, vmem_limit_bytes=60 << 20
        ),
        cost_estimate=pl.CostEstimate(flops=8_300_000_000, bytes_accessed=25_000_000, transcendentals=800_000),
    )(lengths, ln_gain, layer_input, w_query, w_keyval.T, w_output, kv_cache)


def solution(mesh):
    in_specs = (
        P("gy", "gx"),
        P("gx"),
        P("gx", "gy"),
        P("gx", "gy"),
        P("gy", "gx"),
        P(("gx", "gy"), None, None),
        P(("gx", "gy")),
    )
    out_specs = P("gy", "gx")
    return jax.shard_map(local, mesh=mesh, in_specs=in_specs, out_specs=out_specs, check_vma=False)
```

```python
import functools

import jax
import jax.numpy as jnp
from jax import lax
from jax.experimental import pallas as pl
from jax.experimental.pallas import tpu as pltpu
from jax.sharding import PartitionSpec as P

MESH = pl.DeviceIdType.MESH
F32 = jnp.float32
BF16 = jnp.bfloat16

HQ = 48
HS = 256
D = 18432
FEATURES = 2304
COLS = 768
KV = 32
CACHE = 2048
ROWS = 64
PAIR = 128
HALF = 400
LAST = 144
OUT = 2304


FAR_FIRST = (12, 4, 11, 13, 5, 3, 10, 14, 6, 2, 8, 9, 7, 15, 1)


class Ring:
    def __init__(self, device, pos, partner):
        self.device, self.pos, self.partner = device, pos, partner

    def near(self, step):
        return self.device(0, step)

    def across(self):
        return self.device(1, 0)


def taken(ref, sem):
    pltpu.make_async_copy(ref, ref, sem).wait()


def gather_plan(ring, slot, ref, half, send, recvs):
    def whole(i, dz, dr, target):
        place = slot(dz, dr)
        return pltpu.make_async_remote_copy(
            ref.at[place], ref.at[place], send, recvs.at[i], device_id=target, device_id_type=MESH
        )

    def part(i, dz, dr, h, target):
        place = slot(dz, dr)
        piece = ref.at[place, pl.ds(h * half, half)]
        return pltpu.make_async_remote_copy(
            piece, piece, send, recvs.at[i], device_id=target, device_id_type=MESH
        )

    up, down, across = ring.near(1), ring.near(-1), ring.across()
    outgoing = [
        lambda: part(0, 0, 0, 0, across),
        lambda: part(1, 0, 0, 1, across),
        lambda: whole(2, 0, 0, up),
        lambda: whole(3, 0, 0, down),
        lambda: part(4, 1, 0, 0, up),
        lambda: part(5, 1, 0, 0, down),
        lambda: part(6, 1, 0, 1, up),
        lambda: part(7, 1, 0, 1, down),
        lambda: part(8, 0, -1, 0, up),
        lambda: part(9, 0, 1, 1, down),
        lambda: part(10, 1, -1, 0, up),
        lambda: part(11, 1, 1, 1, down),
    ]
    incoming = [
        lambda: part(0, 1, 0, 0, across),
        lambda: part(1, 1, 0, 1, across),
        lambda: whole(2, 0, -1, up),
        lambda: whole(3, 0, 1, down),
        lambda: part(4, 1, -1, 0, up),
        lambda: part(5, 1, 1, 0, down),
        lambda: part(6, 1, -1, 1, up),
        lambda: part(7, 1, 1, 1, down),
        lambda: part(8, 0, 2, 0, up),
        lambda: part(9, 0, 2, 1, down),
        lambda: part(10, 1, 2, 0, up),
        lambda: part(11, 1, 2, 1, down),
    ]
    return outgoing, incoming


def arrival(s):
    dz = jnp.where((s == 1) | (s == 4) | (s == 5) | (s == 7), 1, 0)
    dr = jnp.where((s == 2) | (s == 4), 3, jnp.where((s == 3) | (s == 5), 1, jnp.where(s >= 6, 2, 0)))
    return dz, dr


class Reduce:
    def __init__(self, ring, part, far, mid, zsend, zrecv, keep, sems):
        self.ring, self.part, self.far, self.mid = ring, part, far, mid
        self.zsend, self.zrecv, self.keep = zsend, zrecv, keep
        self.send, self.far_recv, self.mid_recv, self.z_send, self.z_recv = sems

    def role(self, r):
        return lax.rem(r - self.ring.pos + 4, 4)

    def far_copy(self, k, z, p, h):
        target = self.ring.near(1 - 2 * h)
        return pltpu.make_async_remote_copy(
            self.part(k, p, h), self.far(z, h, p), self.send, self.far_recv.at[z, h, p],
            device_id=target, device_id_type=MESH,
        )

    def mid_copy(self, k, z, p, d, h):
        target = self.ring.near(1 - 2 * d)
        return pltpu.make_async_remote_copy(
            self.part(k, p, h), self.mid(z, d, p, h), self.send, self.mid_recv.at[z, d, p],
            device_id=target, device_id_type=MESH,
        )

    def z_copy(self, p, h):
        return pltpu.make_async_remote_copy(
            self.zsend(p, h), self.zrecv(p, h), self.z_send, self.z_recv.at[p],
            device_id=self.ring.across(), device_id_type=MESH,
        )

    def first(self, k, z, r, p):
        role = self.role(r)

        @pl.when(role == 2)
        def _():
            self.far_copy(k, z, p, 0).start()
            self.far_copy(k, z, p, 1).start()

        @pl.when(lax.rem(role, 2) == 1)
        def _():
            d = role // 2
            self.mid_copy(k, z, p, d, 1 - d).start()

    def second(self, k, z, r):
        role = self.role(r)

        @pl.when(lax.rem(role, 2) == 1)
        def _():
            d = role // 2
            for p in range(3):
                self.far_copy(k, z, p, d).wait_recv()
                piece = self.part(k, p, d)
                piece[...] = (piece[...].astype(F32) + self.far(z, d, p)[...].astype(F32)).astype(BF16)
                self.mid_copy(k, z, p, d, d).start()

    def third(self, k, z, r):
        role = self.role(r)

        def total(p, h):
            sums = self.mid(z, 0, p, h)[...].astype(F32) + self.mid(z, 1, p, h)[...].astype(F32)
            return self.part(k, p, h)[...].astype(F32) + sums

        @pl.when(role == 0)
        def _():
            for p in range(3):
                for d in range(2):
                    taken(self.mid(z, d, p, None), self.mid_recv.at[z, d, p])

                @pl.when(z != self.ring.partner)
                def _():
                    for h in range(2):
                        self.zsend(p, h)[...] = total(p, h).astype(BF16)
                        self.z_copy(p, h).start()

                @pl.when(z == self.ring.partner)
                def _():
                    for h in range(2):
                        self.keep(p, h)[...] = total(p, h)

    def result(self, p):
        taken(self.zrecv(p, None), self.z_recv.at[p])
        return [self.keep(p, h)[...] + self.zrecv(p, h)[...].astype(F32) for h in range(2)]

    def finish(self, six_blocks, one_block):
        taken(six_blocks, self.send)
        taken(one_block, self.z_send)


def run(f):
    def body(i, carry):
        f(i)
        return carry

    return body


def loop(start, stop, f):
    lax.fori_loop(start, stop, run(f), 0)


def to_columns(rows):
    return jnp.concatenate([rows] * 16, axis=0).T


def kernel(
    lengths_hbm, gain_hbm, x_hbm, wq_hbm, wkv_hbm, wo_hbm, kv_hbm, out_hbm,
    lengths, gain, out,
    xbuf, lhs, wq, wkv, wo, kv, stat_send, stats, row_stats,
    part1, far1, mid1, zsend1, zrecv1, keep1,
    asend, arecv, qf, new_kv, scores, osf, osend, orecv,
    abuf, tbuf, sib, far2, mid2, zsend2, zrecv2, keep2,
    load_sems, out_sems, stat_s, stat_r, row_s, row_r, ag1_s, ag1_r, core1_s, core1_r,
    send1, far1_r, mid1_r, z1_s, z1_r, a_s, a_r, o_s, o_r, ag2_s, ag2_r, core2_s, core2_r,
    send2, far2_r, mid2_r, z2_s, z2_r,
):
    gx, gy = lax.axis_index("gx"), lax.axis_index("gy")
    x, zh = gx // 2, lax.rem(gx, 2)
    zl, y, c = gy // 8, lax.rem(gy // 2, 4), lax.rem(gy, 2)

    loads = [
        pltpu.make_async_copy(x_hbm, xbuf.at[gy], load_sems.at[0]),
        pltpu.make_async_copy(wq_hbm, wq, load_sems.at[1]),
        pltpu.make_async_copy(wkv_hbm, wkv, load_sems.at[2]),
        pltpu.make_async_copy(kv_hbm, kv, load_sems.at[3]),
        pltpu.make_async_copy(wo_hbm, wo, load_sems.at[4]),
        pltpu.make_async_copy(gain_hbm, gain, load_sems.at[5]),
        pltpu.make_async_copy(lengths_hbm, lengths, load_sems.at[6]),
    ]
    loads[0].start()

    barrier = pltpu.get_barrier_semaphore()

    def greet(target):
        pl.semaphore_signal(barrier, inc=1, device_id=target, device_id_type=MESH)

    loop(1, 8, lambda i: greet((lax.rem(gx + i, 8), gy)))
    loop(1, 16, lambda i: greet((gx, lax.rem(gy + i, 16))))

    def y_device(dz, dr):
        return (gx, (lax.rem(zl + dz, 2) * 4 + lax.rem(y + dr + 4, 4)) * 2 + c)

    def x_device(dz, dr):
        return (lax.rem(x + dr + 4, 4) * 2 + lax.rem(zh + dz, 2), gy)

    sibling = (gx, gy + 1 - 2 * c)
    y_ring = Ring(y_device, y, zl)
    x_ring = Ring(x_device, x, zh)

    loads[0].wait()
    for load in loads[1:]:
        load.start()
    row = xbuf[gy].astype(F32)
    sums = jnp.sum(row, axis=1, keepdims=True)
    squares = jnp.sum(row * row, axis=1, keepdims=True)
    lane = lax.broadcasted_iota(jnp.int32, (ROWS, 128), 1)
    tall = jnp.where(lane == 0, sums, jnp.where(lane == 1, squares, 0.0))
    stat_send[...] = jnp.concatenate([tall, tall], axis=0).T[0:8]
    stats[gx] = stat_send[...]

    pl.semaphore_wait(barrier, 22)

    def y_slot(dz, dr):
        return y_device(dz, dr)[1]

    out1, in1 = gather_plan(y_ring, y_slot, xbuf, ROWS // 2, ag1_s.at[0], ag1_r)

    def core_copy1(i, dz, dr):
        place = y_slot(dz, dr)
        return pltpu.make_async_remote_copy(
            xbuf.at[place], xbuf.at[place], core1_s.at[0], core1_r.at[i], device_id=sibling, device_id_type=MESH
        )

    def core_arrived1(i, dz, dr):
        place = y_slot(dz, dr) + 1 - 2 * c
        return pltpu.make_async_remote_copy(
            xbuf.at[place], xbuf.at[place], core1_s.at[0], core1_r.at[i], device_id=sibling, device_id_type=MESH
        )

    def stat_copy(i, slot):
        return pltpu.make_async_remote_copy(
            stat_send, stats.at[slot], stat_s.at[0], stat_r.at[0],
            device_id=(lax.rem(gx + i, 8), gy), device_id_type=MESH,
        )

    def row_copy(i, slot):
        return pltpu.make_async_remote_copy(
            row_stats.at[slot], row_stats.at[slot], row_s.at[0], row_r.at[i],
            device_id=(gx, lax.rem(gy + i, 16)), device_id_type=MESH,
        )

    loop(1, 8, lambda i: stat_copy(i, gx).start())
    for i in range(4):
        out1[i]().start()
    core_copy1(0, 0, 0).start()

    taken(stats.at[pl.ds(0, 7)], stat_r.at[0])
    total = jnp.sum(stats[...], axis=0)
    average = total[0:1] * (1.0 / D)
    variance = total[1:2] * (1.0 / D) - average * average
    deviation = lax.rsqrt(variance + 1e-05)
    row_stats[gy] = jnp.concatenate([average, deviation, jnp.zeros((6, 128), F32)], axis=0)
    for i in FAR_FIRST:
        row_copy(i, gy).start()

    def rows1(p):
        return pl.ds(128 * p, LAST if p == 2 else 128)

    def both(h):
        return pl.ds(0, 2) if h is None else h

    reduce1 = Reduce(
        x_ring,
        lambda k, p, h: part1.at[k, h, rows1(p)],
        lambda z, d, p: far1.at[z, d, rows1(p)],
        lambda z, d, p, h: mid1.at[z, d, both(h), rows1(p)],
        lambda p, h: zsend1.at[h, rows1(p)],
        lambda p, h: zrecv1.at[both(h), rows1(p)],
        lambda p, h: keep1.at[h, rows1(p)],
        (send1.at[0], far1_r, mid1_r, z1_s.at[0], z1_r),
    )

    def chip1(s):
        dz, dr = arrival(s)
        k = lax.rem(zl + dz, 2) * 4 + lax.rem(y + dr, 4)
        return k, lax.rem(k, 2), k // 2

    def compute1(s):
        k, z, r = chip1(s)
        dz, dr = arrival(s)
        for u in range(2):
            source = 2 * k + u
            i = lax.rem(gy - source + 16, 16)

            @pl.when(i > 0)
            def _():
                row_copy(i, source).wait_recv()

        core_arrived1(s, dz, dr).wait_recv()
        first_lanes = lax.broadcasted_iota(jnp.int32, (8, 128), 1) < ROWS
        columns = to_columns(jnp.where(first_lanes, row_stats[2 * k], row_stats[2 * k + 1]))
        rows = xbuf[pl.ds(2 * k, 2)].reshape(PAIR, FEATURES).astype(F32)
        lhs[...] = ((rows - columns[:, 0:1]) * columns[:, 1:2] * gain[...].reshape(1, FEATURES)).astype(BF16)
        for p in range(3):
            q = jnp.dot(lhs[...], wq[:, p * 256 : (p + 1) * 256], preferred_element_type=F32).astype(BF16)
            for h in range(2):
                part1[k, h, pl.ds(128 * p, 128)] = q[:, h * 128 : (h + 1) * 128]
            if p == 2:
                new = lax.dot_general(
                    wkv[...], lhs[...], (((1,), (1,)), ((), ())), preferred_element_type=F32
                ).astype(BF16)
                for h in range(2):
                    part1[k, h, pl.ds(384, 16)] = new[16 * h : 16 * h + 16]
            reduce1.first(k, z, r, p)

    in1[0]().wait_recv()
    out1[4]().start()
    out1[5]().start()
    in1[1]().wait_recv()
    out1[6]().start()
    out1[7]().start()
    core_copy1(1, 1, 0).start()
    in1[2]().wait_recv()
    out1[8]().start()
    core_copy1(2, 0, -1).start()
    in1[3]().wait_recv()
    out1[9]().start()
    core_copy1(3, 0, 1).start()
    loads[1].wait()
    loads[2].wait()
    loads[5].wait()

    def second1(s):
        reduce1.second(*chip1(s))

    def third1(s):
        reduce1.third(*chip1(s))

    def step1(s):
        @pl.when(s == 4)
        def _():
            in1[4]().wait_recv()
            out1[10]().start()
            in1[7]().wait_recv()
            out1[11]().start()
            in1[6]().wait_recv()
            core_copy1(4, 1, -1).start()
            in1[5]().wait_recv()
            core_copy1(5, 1, 1).start()
            loop(0, 2, second1)

        @pl.when(s == 6)
        def _():
            in1[8]().wait_recv()
            in1[9]().wait_recv()
            core_copy1(6, 0, 2).start()
            loop(2, 4, second1)

        @pl.when(s == 7)
        def _():
            in1[10]().wait_recv()
            in1[11]().wait_recv()
            core_copy1(7, 1, 2).start()
            loop(4, 6, second1)

        compute1(s)

    loop(0, 8, step1)
    loop(0, 4, third1)
    loop(6, 8, second1)
    loop(4, 8, third1)

    final = [reduce1.result(p) for p in range(3)]
    blocks = [final[p][h][0:128].reshape(16, 8, 128) for p in range(3) for h in range(2)]
    fresh = jnp.concatenate([final[2][0][128:144], final[2][1][128:144]] * 4, axis=0).T.reshape(16, 8, 128)
    halves = [jnp.concatenate(blocks[3 * h : 3 * h + 3] + [fresh], axis=2) for h in range(2)]
    asend[...] = jnp.concatenate(halves, axis=1).astype(BF16)
    arecv[gy] = asend[gy]

    def all_to_all(src, dst, ss, rs):
        for i in FAR_FIRST:
            target = lax.rem(gy + i, 16)
            pltpu.make_async_remote_copy(
                src.at[target], dst.at[gy], ss, rs, device_id=(gx, target), device_id_type=MESH
            ).start()
        taken(dst.at[pl.ds(0, 15)], rs)

    all_to_all(asend, arecv, a_s.at[0], a_r.at[0])

    got = arecv[...].astype(F32)
    for b in range(6):
        h, at = b // 3, (b % 3) * 128
        qf[b] = got[:, 8 * h : 8 * h + 8, at : at + 128].reshape(128, 128)
    fresh = got[:, 0:8, 384 : 384 + KV]
    for half in range(2):
        new_kv[:, half * HS : (half + 1) * HS] = jnp.concatenate([fresh[8 * half + g] for g in range(8)], axis=1)
    loads[3].wait()
    loads[6].wait()

    def query(r):
        lanes = [qf[b, pl.ds(r, 16, stride=8), :] for b in range(6)]
        return jnp.concatenate([jnp.concatenate(lanes[2 * j : 2 * j + 2], axis=1) for j in range(3)], axis=0)

    for r in range(8):
        scores[r] = lax.dot_general(
            (query(r) * (HS**-0.5)).astype(BF16), kv[r, :, 0:HS], (((1,), (1,)), ((), ())),
            preferred_element_type=F32,
        )
    slot = lax.broadcasted_iota(jnp.int32, (1, CACHE), 1)
    for r in range(8):
        fresh_row = new_kv[r : r + 1, :]
        score = scores[r] + jnp.where(slot < lengths[r], 0.0, -1e30)
        own = jnp.sum(query(r) * fresh_row[:, 0:HS], axis=1, keepdims=True) * (HS**-0.5)
        top = jnp.maximum(jnp.max(score, axis=1, keepdims=True), own)
        probs = jnp.exp(score - top)
        own_prob = jnp.exp(own - top)
        scale = 1.0 / (jnp.sum(probs, axis=1, keepdims=True) + own_prob)
        mixed = jnp.dot(probs.astype(BF16), kv[r, :, HS : 2 * HS], preferred_element_type=F32)
        mixed = (mixed + own_prob * fresh_row[:, HS : 2 * HS]) * scale
        for b in range(6):
            j, at = b // 2, (b % 2) * 128
            osf[b, pl.ds(r, 16, stride=8), :] = mixed[16 * j : 16 * j + 16, at : at + 128]

    result = [jnp.concatenate([osf[3 * h + b].reshape(16, 8, 128) for b in range(3)], axis=2) for h in range(2)]
    osend[...] = jnp.concatenate(result, axis=1).astype(BF16)
    orecv[gy] = osend[gy]
    all_to_all(osend, orecv, o_s.at[0], o_r.at[0])
    back = orecv[...].astype(F32)
    heads = jnp.concatenate([back[:, 0:8].reshape(PAIR, 384), back[:, 8:16].reshape(PAIR, 384)], axis=1)
    abuf[gx] = heads.astype(BF16)

    def x_slot(dz, dr):
        return x_device(dz, dr)[0]

    out2, in2 = gather_plan(x_ring, x_slot, abuf, PAIR // 2, ag2_s.at[0], ag2_r)
    reduce2 = Reduce(
        y_ring,
        lambda k, p, h: tbuf.at[k, p, c, pl.ds(h * 32, 32)],
        lambda z, d, p: far2.at[z, d, p],
        lambda z, d, p, h: mid2.at[z, d, p, both(h)],
        lambda p, h: zsend2.at[p, h],
        lambda p, h: zrecv2.at[p, both(h)],
        lambda p, h: keep2.at[p, h],
        (send2.at[0], far2_r, mid2_r, z2_s.at[0], z2_r),
    )

    def core_copy2(k, p):
        return pltpu.make_async_remote_copy(
            tbuf.at[k, p, 1 - c], sib.at[k, p], core2_s.at[0], core2_r.at[k, p],
            device_id=sibling, device_id_type=MESH,
        )

    same = jnp.where(x // 2 == zl, 1, 0)
    twin = jnp.where(lax.rem(x, 2) == 0, 1, 3)

    def chip2(s):
        near = jnp.where((s == 3) | (s == 7), twin, 4 - twin)
        dr_same = jnp.where(s < 2, 0, jnp.where((s == 5) | (s == 6), 2, near))
        dz_same = jnp.where((s == 1) | (s == 4) | (s >= 6), 1, 0)
        near = jnp.where((s == 2) | (s == 4), twin, 4 - twin)
        dr_else = jnp.where(s < 2, 0, jnp.where(s >= 6, 2, near))
        dz_else = jnp.where((s == 1) | (s == 4) | (s == 5) | (s == 7), 1, 0)
        dr = same * dr_same + (1 - same) * dr_else
        dz = same * dz_same + (1 - same) * dz_else
        k = lax.rem(x + dr, 4) * 2 + lax.rem(zh + dz, 2)
        return k, k // 4, lax.rem(k, 4)

    for i in range(4):
        out2[i]().start()
    loads[4].wait()

    def first2(s):
        k, z, r = chip2(s)
        for p in range(3):
            core_copy2(k, p).wait_recv()
            tbuf[k, p, c] = (tbuf[k, p, c].astype(F32) + sib[k, p].astype(F32)).astype(BF16)
            reduce2.first(k, z, r, p)

    def second2(s):
        reduce2.second(*chip2(s))

    def third2(s):
        reduce2.third(*chip2(s))

    def step2(s):
        @pl.when(s == 1)
        def _():
            first2(0)
            in2[0]().wait_recv()
            out2[4]().start()
            out2[5]().start()
            in2[1]().wait_recv()
            out2[6]().start()
            out2[7]().start()
            in2[2]().wait_recv()
            in2[3]().wait_recv()

        @pl.when(s == 3)
        def _():
            out2[8]().start()
            out2[9]().start()

        @pl.when(s == 4)
        def _():
            first2(3)
            second2(0)
            in2[4]().wait_recv()
            out2[10]().start()
            in2[7]().wait_recv()
            out2[11]().start()
            in2[6]().wait_recv()
            in2[5]().wait_recv()

        @pl.when(s == 6 - same)
        def _():
            in2[8]().wait_recv()
            in2[9]().wait_recv()

        @pl.when(s == 7 - same)
        def _():
            in2[10]().wait_recv()
            in2[11]().wait_recv()

        k, _, _ = chip2(s)
        rows = abuf[k]
        for p in range(3):
            for t in range(3):
                at = (3 * p + t) * 256
                term = jnp.dot(rows, wo[:, at : at + 256], preferred_element_type=F32).astype(BF16)
                tbuf[k, p, 0, :, t * 256 : (t + 1) * 256] = term[0:ROWS]
                tbuf[k, p, 1, :, t * 256 : (t + 1) * 256] = term[ROWS:PAIR]
            core_copy2(k, p).start()

        @pl.when((s > 1) & (s != 4))
        def _():
            first2(s - 1)

        @pl.when(s >= 4)
        def _():
            second2(s - 3)

        @pl.when(s == 7)
        def _():
            loop(0, 2, third2)

    loop(0, 8, step2)
    first2(7)
    loop(5, 7, second2)
    loop(2, 4, third2)
    second2(7)
    loop(4, 8, third2)
    writes = []
    for p in range(3):
        for h, rows in enumerate(reduce2.result(p)):
            out_hbm[pl.ds(h * 32, 32), p * 768 : (p + 1) * 768] = rows.astype(BF16)

    taken(stats.at[pl.ds(0, 7)], stat_s.at[0])
    taken(row_stats.at[pl.ds(0, 15)], row_s.at[0])
    taken(asend.at[pl.ds(0, 15)], a_s.at[0])
    taken(osend.at[pl.ds(0, 15)], o_s.at[0])
    taken(xbuf.at[pl.ds(0, 7)], ag1_s.at[0])
    taken(abuf.at[pl.ds(0, 7)], ag2_s.at[0])
    taken(xbuf.at[pl.ds(0, 8)], core1_s.at[0])
    taken(sib, core2_s.at[0])
    reduce1.finish(part1.at[pl.ds(0, 6)], zsend1)
    reduce2.finish(tbuf.at[pl.ds(0, 6), :, 0], zsend2)


def local(layer_input, ln_gain, w_query, w_keyval, w_output, kv_cache, lengths):
    any_space = pl.BlockSpec(memory_space=pl.ANY)
    dma = pltpu.SemaphoreType.DMA
    scratch = [
        pltpu.SMEM((8,), jnp.int32),
        pltpu.VMEM((FEATURES,), F32),
        pltpu.VMEM((ROWS, OUT), BF16),
        pltpu.VMEM((16, ROWS, FEATURES), BF16),
        pltpu.VMEM((PAIR, FEATURES), BF16),
        pltpu.VMEM((FEATURES, COLS), BF16),
        pltpu.VMEM((KV, FEATURES), BF16),
        pltpu.VMEM((COLS, OUT), BF16),
        pltpu.VMEM((8, CACHE, 2 * HS), BF16),
        pltpu.VMEM((8, 128), F32),
        pltpu.VMEM((8, 8, 128), F32),
        pltpu.VMEM((16, 8, 128), F32),
        pltpu.VMEM((8, 2, HALF, 128), BF16),
        pltpu.VMEM((2, 2, HALF, 128), BF16),
        pltpu.VMEM((2, 2, 2, HALF, 128), BF16),
        pltpu.VMEM((2, HALF, 128), BF16),
        pltpu.VMEM((2, HALF, 128), BF16),
        pltpu.VMEM((2, HALF, 128), F32),
        pltpu.VMEM((16, 16, 512), BF16),
        pltpu.VMEM((16, 16, 512), BF16),
        pltpu.VMEM((6, 128, 128), F32),
        pltpu.VMEM((8, 2 * HS), F32),
        pltpu.VMEM((8, HQ, CACHE), F32),
        pltpu.VMEM((6, 128, 128), F32),
        pltpu.VMEM((16, 16, 384), BF16),
        pltpu.VMEM((16, 16, 384), BF16),
        pltpu.VMEM((8, PAIR, COLS), BF16),
        pltpu.VMEM((8, 3, 2, ROWS, 768), BF16),
        pltpu.VMEM((8, 3, ROWS, 768), BF16),
        pltpu.VMEM((2, 2, 3, 32, 768), BF16),
        pltpu.VMEM((2, 2, 3, 2, 32, 768), BF16),
        pltpu.VMEM((3, 2, 32, 768), BF16),
        pltpu.VMEM((3, 2, 32, 768), BF16),
        pltpu.VMEM((3, 2, 32, 768), F32),
        dma((7,)), dma((3,)),
        dma((1,)), dma((1,)), dma((1,)), dma((16,)),
        dma((1,)), dma((12,)), dma((1,)), dma((8,)),
        dma((1,)), dma((2, 2, 3)), dma((2, 2, 3)), dma((1,)), dma((3,)),
        dma((1,)), dma((1,)), dma((1,)), dma((1,)),
        dma((1,)), dma((12,)), dma((1,)), dma((8, 3)),
        dma((1,)), dma((2, 2, 3)), dma((2, 2, 3)), dma((1,)), dma((3,)),
    ]
    return pl.pallas_call(
        kernel,
        name="decode_attention",
        out_shape=pltpu.VMEM((ROWS, OUT), BF16),
        in_specs=[any_space] * 7,
        out_specs=pl.BlockSpec(memory_space=pltpu.VMEM),
        scratch_shapes=scratch,
        compiler_params=pltpu.CompilerParams(
            collective_id=0, has_side_effects=True, vmem_limit_bytes=60 << 20
        ),
        cost_estimate=pl.CostEstimate(flops=8_300_000_000, bytes_accessed=25_000_000, transcendentals=800_000),
    )(lengths, ln_gain, layer_input, w_query, w_keyval.T, w_output, kv_cache)


def solution(mesh):
    in_specs = (
        P("gy", "gx"),
        P("gx"),
        P("gx", "gy"),
        P("gx", "gy"),
        P("gy", "gx"),
        P(("gx", "gy"), None, None),
        P(("gx", "gy")),
    )
    out_specs = P("gy", "gx")
    return jax.shard_map(local, mesh=mesh, in_specs=in_specs, out_specs=out_specs, check_vma=False)
```

```python
import functools

import jax
import jax.numpy as jnp
from jax import lax
from jax.experimental import pallas as pl
from jax.experimental.pallas import tpu as pltpu
from jax.sharding import PartitionSpec as P

MESH = pl.DeviceIdType.MESH
F32 = jnp.float32
BF16 = jnp.bfloat16

HQ = 48
HS = 256
D = 18432
FEATURES = 2304
COLS = 768
KV = 32
CACHE = 2048
ROWS = 64
PAIR = 128
HALF = 400
LAST = 144
OUT = 2304


FAR_FIRST = (12, 4, 11, 13, 5, 3, 10, 14, 6, 2, 8, 9, 7, 15, 1)


class Ring:
    def __init__(self, device, pos, partner):
        self.device, self.pos, self.partner = device, pos, partner

    def near(self, step):
        return self.device(0, step)

    def across(self):
        return self.device(1, 0)


def taken(ref, sem):
    pltpu.make_async_copy(ref, ref, sem).wait()


def gather_plan(ring, slot, ref, half, send, recvs):
    def whole(i, dz, dr, target):
        place = slot(dz, dr)
        return pltpu.make_async_remote_copy(
            ref.at[place], ref.at[place], send, recvs.at[i], device_id=target, device_id_type=MESH
        )

    def part(i, dz, dr, h, target):
        place = slot(dz, dr)
        piece = ref.at[place, pl.ds(h * half, half)]
        return pltpu.make_async_remote_copy(
            piece, piece, send, recvs.at[i], device_id=target, device_id_type=MESH
        )

    up, down, across = ring.near(1), ring.near(-1), ring.across()
    outgoing = [
        lambda: part(0, 0, 0, 0, across),
        lambda: part(1, 0, 0, 1, across),
        lambda: whole(2, 0, 0, up),
        lambda: whole(3, 0, 0, down),
        lambda: part(4, 1, 0, 0, up),
        lambda: part(5, 1, 0, 0, down),
        lambda: part(6, 1, 0, 1, up),
        lambda: part(7, 1, 0, 1, down),
        lambda: part(8, 0, -1, 0, up),
        lambda: part(9, 0, 1, 1, down),
        lambda: part(10, 1, -1, 0, up),
        lambda: part(11, 1, 1, 1, down),
    ]
    incoming = [
        lambda: part(0, 1, 0, 0, across),
        lambda: part(1, 1, 0, 1, across),
        lambda: whole(2, 0, -1, up),
        lambda: whole(3, 0, 1, down),
        lambda: part(4, 1, -1, 0, up),
        lambda: part(5, 1, 1, 0, down),
        lambda: part(6, 1, -1, 1, up),
        lambda: part(7, 1, 1, 1, down),
        lambda: part(8, 0, 2, 0, up),
        lambda: part(9, 0, 2, 1, down),
        lambda: part(10, 1, 2, 0, up),
        lambda: part(11, 1, 2, 1, down),
    ]
    return outgoing, incoming


def arrival(s):
    dz = jnp.where((s == 1) | (s == 4) | (s == 5) | (s == 7), 1, 0)
    dr = jnp.where((s == 2) | (s == 4), 3, jnp.where((s == 3) | (s == 5), 1, jnp.where(s >= 6, 2, 0)))
    return dz, dr


class Reduce:
    def __init__(self, ring, part, far, mid, zsend, zrecv, keep, sems):
        self.ring, self.part, self.far, self.mid = ring, part, far, mid
        self.zsend, self.zrecv, self.keep = zsend, zrecv, keep
        self.send, self.far_recv, self.mid_recv, self.z_send, self.z_recv = sems

    def role(self, r):
        return lax.rem(r - self.ring.pos + 4, 4)

    def far_copy(self, k, z, p, h):
        target = self.ring.near(1 - 2 * h)
        return pltpu.make_async_remote_copy(
            self.part(k, p, h), self.far(z, h, p), self.send, self.far_recv.at[z, h, p],
            device_id=target, device_id_type=MESH,
        )

    def mid_copy(self, k, z, p, d, h):
        target = self.ring.near(1 - 2 * d)
        return pltpu.make_async_remote_copy(
            self.part(k, p, h), self.mid(z, d, p, h), self.send, self.mid_recv.at[z, d, p],
            device_id=target, device_id_type=MESH,
        )

    def z_copy(self, p, h):
        return pltpu.make_async_remote_copy(
            self.zsend(p, h), self.zrecv(p, h), self.z_send, self.z_recv.at[p],
            device_id=self.ring.across(), device_id_type=MESH,
        )

    def first(self, k, z, r, p):
        role = self.role(r)

        @pl.when(role == 2)
        def _():
            self.far_copy(k, z, p, 0).start()
            self.far_copy(k, z, p, 1).start()

        @pl.when(lax.rem(role, 2) == 1)
        def _():
            d = role // 2
            self.mid_copy(k, z, p, d, 1 - d).start()

    def second(self, k, z, r):
        role = self.role(r)

        @pl.when(lax.rem(role, 2) == 1)
        def _():
            d = role // 2
            for p in range(3):
                self.far_copy(k, z, p, d).wait_recv()
                piece = self.part(k, p, d)
                piece[...] = (piece[...].astype(F32) + self.far(z, d, p)[...].astype(F32)).astype(BF16)
                self.mid_copy(k, z, p, d, d).start()

    def third(self, k, z, r):
        role = self.role(r)

        def total(p, h):
            sums = self.mid(z, 0, p, h)[...].astype(F32) + self.mid(z, 1, p, h)[...].astype(F32)
            return self.part(k, p, h)[...].astype(F32) + sums

        @pl.when(role == 0)
        def _():
            for p in range(3):
                for d in range(2):
                    taken(self.mid(z, d, p, None), self.mid_recv.at[z, d, p])

                @pl.when(z != self.ring.partner)
                def _():
                    for h in range(2):
                        self.zsend(p, h)[...] = total(p, h).astype(BF16)
                        self.z_copy(p, h).start()

                @pl.when(z == self.ring.partner)
                def _():
                    for h in range(2):
                        self.keep(p, h)[...] = total(p, h)

    def result(self, p):
        taken(self.zrecv(p, None), self.z_recv.at[p])
        return [self.keep(p, h)[...] + self.zrecv(p, h)[...].astype(F32) for h in range(2)]

    def finish(self, six_blocks, one_block):
        taken(six_blocks, self.send)
        taken(one_block, self.z_send)


def run(f):
    def body(i, carry):
        f(i)
        return carry

    return body


def loop(start, stop, f):
    lax.fori_loop(start, stop, run(f), 0)


def to_columns(rows):
    return jnp.concatenate([rows] * 16, axis=0).T


def kernel(
    lengths_hbm, gain_hbm, x_hbm, wq_hbm, wkv_hbm, wo_hbm, kv_hbm, out_hbm,
    lengths, gain, out,
    xbuf, lhs, wq, wkv, wo, kv, stat_send, stats, row_stats,
    part1, far1, mid1, zsend1, zrecv1, keep1,
    asend, arecv, qf, new_kv, scores, osf, osend, orecv,
    abuf, tbuf, sib, far2, mid2, zsend2, zrecv2, keep2,
    load_sems, out_sems, stat_s, stat_r, row_s, row_r, ag1_s, ag1_r, core1_s, core1_r,
    send1, far1_r, mid1_r, z1_s, z1_r, a_s, a_r, o_s, o_r, ag2_s, ag2_r, core2_s, core2_r,
    send2, far2_r, mid2_r, z2_s, z2_r,
):
    gx, gy = lax.axis_index("gx"), lax.axis_index("gy")
    x, zh = gx // 2, lax.rem(gx, 2)
    zl, y, c = gy // 8, lax.rem(gy // 2, 4), lax.rem(gy, 2)

    loads = [
        pltpu.make_async_copy(x_hbm, xbuf.at[gy], load_sems.at[0]),
        pltpu.make_async_copy(wq_hbm, wq, load_sems.at[1]),
        pltpu.make_async_copy(wkv_hbm, wkv, load_sems.at[2]),
        pltpu.make_async_copy(kv_hbm, kv, load_sems.at[3]),
        pltpu.make_async_copy(wo_hbm, wo, load_sems.at[4]),
        pltpu.make_async_copy(gain_hbm, gain, load_sems.at[5]),
        pltpu.make_async_copy(lengths_hbm, lengths, load_sems.at[6]),
    ]
    loads[0].start()

    barrier = pltpu.get_barrier_semaphore()

    def greet(target):
        pl.semaphore_signal(barrier, inc=1, device_id=target, device_id_type=MESH)

    loop(1, 8, lambda i: greet((lax.rem(gx + i, 8), gy)))
    loop(1, 16, lambda i: greet((gx, lax.rem(gy + i, 16))))

    def y_device(dz, dr):
        return (gx, (lax.rem(zl + dz, 2) * 4 + lax.rem(y + dr + 4, 4)) * 2 + c)

    def x_device(dz, dr):
        return (lax.rem(x + dr + 4, 4) * 2 + lax.rem(zh + dz, 2), gy)

    sibling = (gx, gy + 1 - 2 * c)
    y_ring = Ring(y_device, y, zl)
    x_ring = Ring(x_device, x, zh)

    loads[0].wait()
    for load in loads[1:]:
        load.start()
    row = xbuf[gy].astype(F32)
    sums = jnp.sum(row, axis=1, keepdims=True)
    squares = jnp.sum(row * row, axis=1, keepdims=True)
    lane = lax.broadcasted_iota(jnp.int32, (ROWS, 128), 1)
    tall = jnp.where(lane == 0, sums, jnp.where(lane == 1, squares, 0.0))
    stat_send[...] = jnp.concatenate([tall, tall], axis=0).T[0:8]
    stats[gx] = stat_send[...]

    pl.semaphore_wait(barrier, 22)

    def y_slot(dz, dr):
        return y_device(dz, dr)[1]

    out1, in1 = gather_plan(y_ring, y_slot, xbuf, ROWS // 2, ag1_s.at[0], ag1_r)

    def core_copy1(i, dz, dr):
        place = y_slot(dz, dr)
        return pltpu.make_async_remote_copy(
            xbuf.at[place], xbuf.at[place], core1_s.at[0], core1_r.at[i], device_id=sibling, device_id_type=MESH
        )

    def core_arrived1(i, dz, dr):
        place = y_slot(dz, dr) + 1 - 2 * c
        return pltpu.make_async_remote_copy(
            xbuf.at[place], xbuf.at[place], core1_s.at[0], core1_r.at[i], device_id=sibling, device_id_type=MESH
        )

    def stat_copy(i, slot):
        return pltpu.make_async_remote_copy(
            stat_send, stats.at[slot], stat_s.at[0], stat_r.at[0],
            device_id=(lax.rem(gx + i, 8), gy), device_id_type=MESH,
        )

    def row_copy(i, slot):
        return pltpu.make_async_remote_copy(
            row_stats.at[slot], row_stats.at[slot], row_s.at[0], row_r.at[i],
            device_id=(gx, lax.rem(gy + i, 16)), device_id_type=MESH,
        )

    loop(1, 8, lambda i: stat_copy(i, gx).start())
    for i in range(4):
        out1[i]().start()
    core_copy1(0, 0, 0).start()

    taken(stats.at[pl.ds(0, 7)], stat_r.at[0])
    total = jnp.sum(stats[...], axis=0)
    average = total[0:1] * (1.0 / D)
    variance = total[1:2] * (1.0 / D) - average * average
    deviation = lax.rsqrt(variance + 1e-05)
    row_stats[gy] = jnp.concatenate([average, deviation, jnp.zeros((6, 128), F32)], axis=0)
    for i in FAR_FIRST:
        row_copy(i, gy).start()

    def rows1(p):
        return pl.ds(128 * p, LAST if p == 2 else 128)

    def both(h):
        return pl.ds(0, 2) if h is None else h

    reduce1 = Reduce(
        x_ring,
        lambda k, p, h: part1.at[k, h, rows1(p)],
        lambda z, d, p: far1.at[z, d, rows1(p)],
        lambda z, d, p, h: mid1.at[z, d, both(h), rows1(p)],
        lambda p, h: zsend1.at[h, rows1(p)],
        lambda p, h: zrecv1.at[both(h), rows1(p)],
        lambda p, h: keep1.at[h, rows1(p)],
        (send1.at[0], far1_r, mid1_r, z1_s.at[0], z1_r),
    )

    def chip1(s):
        dz, dr = arrival(s)
        k = lax.rem(zl + dz, 2) * 4 + lax.rem(y + dr, 4)
        return k, lax.rem(k, 2), k // 2

    def compute1(s):
        k, z, r = chip1(s)
        dz, dr = arrival(s)
        for u in range(2):
            source = 2 * k + u
            i = lax.rem(gy - source + 16, 16)

            @pl.when(i > 0)
            def _():
                row_copy(i, source).wait_recv()

        core_arrived1(s, dz, dr).wait_recv()
        first_lanes = lax.broadcasted_iota(jnp.int32, (8, 128), 1) < ROWS
        columns = to_columns(jnp.where(first_lanes, row_stats[2 * k], row_stats[2 * k + 1]))
        rows = xbuf[pl.ds(2 * k, 2)].reshape(PAIR, FEATURES).astype(F32)
        lhs[...] = ((rows - columns[:, 0:1]) * columns[:, 1:2] * gain[...].reshape(1, FEATURES)).astype(BF16)
        for p in range(3):
            q = jnp.dot(lhs[...], wq[:, p * 256 : (p + 1) * 256], preferred_element_type=F32).astype(BF16)
            for h in range(2):
                part1[k, h, pl.ds(128 * p, 128)] = q[:, h * 128 : (h + 1) * 128]
            if p == 2:
                new = lax.dot_general(
                    wkv[...], lhs[...], (((1,), (1,)), ((), ())), preferred_element_type=F32
                ).astype(BF16)
                for h in range(2):
                    part1[k, h, pl.ds(384, 16)] = new[16 * h : 16 * h + 16]
            reduce1.first(k, z, r, p)

    in1[0]().wait_recv()
    out1[4]().start()
    out1[5]().start()
    in1[1]().wait_recv()
    out1[6]().start()
    out1[7]().start()
    core_copy1(1, 1, 0).start()
    in1[2]().wait_recv()
    out1[8]().start()
    core_copy1(2, 0, -1).start()
    in1[3]().wait_recv()
    out1[9]().start()
    core_copy1(3, 0, 1).start()
    loads[1].wait()
    loads[2].wait()
    loads[5].wait()

    def second1(s):
        reduce1.second(*chip1(s))

    def third1(s):
        reduce1.third(*chip1(s))

    def step1(s):
        @pl.when(s == 4)
        def _():
            in1[4]().wait_recv()
            out1[10]().start()
            in1[7]().wait_recv()
            out1[11]().start()
            in1[6]().wait_recv()
            core_copy1(4, 1, -1).start()
            in1[5]().wait_recv()
            core_copy1(5, 1, 1).start()
            loop(0, 2, second1)

        @pl.when(s == 6)
        def _():
            in1[8]().wait_recv()
            in1[9]().wait_recv()
            core_copy1(6, 0, 2).start()
            loop(2, 4, second1)

        @pl.when(s == 7)
        def _():
            in1[10]().wait_recv()
            in1[11]().wait_recv()
            core_copy1(7, 1, 2).start()
            loop(4, 6, second1)

        compute1(s)

    loop(0, 8, step1)
    loop(0, 4, third1)
    loop(6, 8, second1)
    loop(4, 8, third1)

    final = [reduce1.result(p) for p in range(3)]
    blocks = [final[p][h][0:128].reshape(16, 8, 128) for p in range(3) for h in range(2)]
    fresh = jnp.concatenate([final[2][0][128:144], final[2][1][128:144]] * 4, axis=0).T.reshape(16, 8, 128)
    halves = [jnp.concatenate(blocks[3 * h : 3 * h + 3] + [fresh], axis=2) for h in range(2)]
    asend[...] = jnp.concatenate(halves, axis=1).astype(BF16)
    arecv[gy] = asend[gy]

    def all_to_all(src, dst, ss, rs):
        for i in FAR_FIRST:
            target = lax.rem(gy + i, 16)
            pltpu.make_async_remote_copy(
                src.at[target], dst.at[gy], ss, rs, device_id=(gx, target), device_id_type=MESH
            ).start()
        taken(dst.at[pl.ds(0, 15)], rs)

    all_to_all(asend, arecv, a_s.at[0], a_r.at[0])

    got = arecv[...].astype(F32)
    for b in range(6):
        h, at = b // 3, (b % 3) * 128
        qf[b] = got[:, 8 * h : 8 * h + 8, at : at + 128].reshape(128, 128)
    fresh = got[:, 0:8, 384 : 384 + KV]
    for half in range(2):
        new_kv[:, half * HS : (half + 1) * HS] = jnp.concatenate([fresh[8 * half + g] for g in range(8)], axis=1)
    loads[3].wait()
    loads[6].wait()

    def query(r):
        lanes = [qf[b, pl.ds(r, 16, stride=8), :] for b in range(6)]
        return jnp.concatenate([jnp.concatenate(lanes[2 * j : 2 * j + 2], axis=1) for j in range(3)], axis=0)

    for r in range(8):
        scores[r] = lax.dot_general(
            (query(r) * (HS**-0.5)).astype(BF16), kv[r, :, 0:HS], (((1,), (1,)), ((), ())),
            preferred_element_type=F32,
        )
    slot = lax.broadcasted_iota(jnp.int32, (1, CACHE), 1)
    for r in range(8):
        fresh_row = new_kv[r : r + 1, :]
        score = scores[r] + jnp.where(slot < lengths[r], 0.0, -1e30)
        own = jnp.sum(query(r) * fresh_row[:, 0:HS], axis=1, keepdims=True) * (HS**-0.5)
        top = jnp.maximum(jnp.max(score, axis=1, keepdims=True), own)
        probs = jnp.exp(score - top)
        own_prob = jnp.exp(own - top)
        scale = 1.0 / (jnp.sum(probs, axis=1, keepdims=True) + own_prob)
        mixed = jnp.dot(probs.astype(BF16), kv[r, :, HS : 2 * HS], preferred_element_type=F32)
        mixed = (mixed + own_prob * fresh_row[:, HS : 2 * HS]) * scale
        for b in range(6):
            j, at = b // 2, (b % 2) * 128
            osf[b, pl.ds(r, 16, stride=8), :] = mixed[16 * j : 16 * j + 16, at : at + 128]

    result = [jnp.concatenate([osf[3 * h + b].reshape(16, 8, 128) for b in range(3)], axis=2) for h in range(2)]
    osend[...] = jnp.concatenate(result, axis=1).astype(BF16)
    orecv[gy] = osend[gy]
    all_to_all(osend, orecv, o_s.at[0], o_r.at[0])
    back = orecv[...].astype(F32)
    heads = jnp.concatenate([back[:, 0:8].reshape(PAIR, 384), back[:, 8:16].reshape(PAIR, 384)], axis=1)
    abuf[gx] = heads.astype(BF16)

    def x_slot(dz, dr):
        return x_device(dz, dr)[0]

    out2, in2 = gather_plan(x_ring, x_slot, abuf, PAIR // 2, ag2_s.at[0], ag2_r)
    reduce2 = Reduce(
        y_ring,
        lambda k, p, h: tbuf.at[k, p, c, pl.ds(h * 32, 32)],
        lambda z, d, p: far2.at[z, d, p],
        lambda z, d, p, h: mid2.at[z, d, p, both(h)],
        lambda p, h: zsend2.at[p, h],
        lambda p, h: zrecv2.at[p, both(h)],
        lambda p, h: keep2.at[p, h],
        (send2.at[0], far2_r, mid2_r, z2_s.at[0], z2_r),
    )

    def core_copy2(k, p):
        return pltpu.make_async_remote_copy(
            tbuf.at[k, p, 1 - c], sib.at[k, p], core2_s.at[0], core2_r.at[k, p],
            device_id=sibling, device_id_type=MESH,
        )

    same = jnp.where(x // 2 == zl, 1, 0)
    twin = jnp.where(lax.rem(x, 2) == 0, 1, 3)

    def chip2(s):
        near = jnp.where((s == 3) | (s == 7), twin, 4 - twin)
        dr_same = jnp.where(s < 2, 0, jnp.where((s == 5) | (s == 6), 2, near))
        dz_same = jnp.where((s == 1) | (s == 4) | (s >= 6), 1, 0)
        near = jnp.where((s == 2) | (s == 4), twin, 4 - twin)
        dr_else = jnp.where(s < 2, 0, jnp.where(s >= 6, 2, near))
        dz_else = jnp.where((s == 1) | (s == 4) | (s == 5) | (s == 7), 1, 0)
        dr = same * dr_same + (1 - same) * dr_else
        dz = same * dz_same + (1 - same) * dz_else
        k = lax.rem(x + dr, 4) * 2 + lax.rem(zh + dz, 2)
        return k, k // 4, lax.rem(k, 4)

    for i in range(4):
        out2[i]().start()
    loads[4].wait()

    def first2(s):
        k, z, r = chip2(s)
        for p in range(3):
            core_copy2(k, p).wait_recv()
            tbuf[k, p, c] = (tbuf[k, p, c].astype(F32) + sib[k, p].astype(F32)).astype(BF16)
            reduce2.first(k, z, r, p)

    def second2(s):
        reduce2.second(*chip2(s))

    def third2(s):
        reduce2.third(*chip2(s))

    def step2(s):
        @pl.when(s == 1)
        def _():
            first2(0)
            in2[0]().wait_recv()
            out2[4]().start()
            out2[5]().start()
            in2[1]().wait_recv()
            out2[6]().start()
            out2[7]().start()
            in2[2]().wait_recv()
            in2[3]().wait_recv()

        @pl.when(s == 3)
        def _():
            out2[8]().start()
            out2[9]().start()

        @pl.when(s == 4)
        def _():
            first2(3)
            in2[4]().wait_recv()
            out2[10]().start()
            in2[7]().wait_recv()
            out2[11]().start()
            in2[6]().wait_recv()
            in2[5]().wait_recv()
            second2(0)

        @pl.when(s == 6 - same)
        def _():
            in2[8]().wait_recv()
            in2[9]().wait_recv()

        @pl.when(s == 7 - same)
        def _():
            in2[10]().wait_recv()
            in2[11]().wait_recv()

        k, _, _ = chip2(s)
        rows = abuf[k]
        for p in range(3):
            for t in range(3):
                at = (3 * p + t) * 256
                term = jnp.dot(rows, wo[:, at : at + 256], preferred_element_type=F32).astype(BF16)
                tbuf[k, p, 0, :, t * 256 : (t + 1) * 256] = term[0:ROWS]
                tbuf[k, p, 1, :, t * 256 : (t + 1) * 256] = term[ROWS:PAIR]
            core_copy2(k, p).start()

        @pl.when((s > 1) & (s != 4))
        def _():
            first2(s - 1)

        @pl.when(s >= 4)
        def _():
            second2(s - 3)

        @pl.when(s == 7)
        def _():
            loop(0, 2, third2)

    loop(0, 8, step2)
    first2(7)
    loop(5, 7, second2)
    loop(2, 4, third2)
    second2(7)
    loop(4, 8, third2)
    writes = []
    for p in range(3):
        for h, rows in enumerate(reduce2.result(p)):
            out_hbm[pl.ds(h * 32, 32), p * 768 : (p + 1) * 768] = rows.astype(BF16)

    taken(stats.at[pl.ds(0, 7)], stat_s.at[0])
    taken(row_stats.at[pl.ds(0, 15)], row_s.at[0])
    taken(asend.at[pl.ds(0, 15)], a_s.at[0])
    taken(osend.at[pl.ds(0, 15)], o_s.at[0])
    taken(xbuf.at[pl.ds(0, 7)], ag1_s.at[0])
    taken(abuf.at[pl.ds(0, 7)], ag2_s.at[0])
    taken(xbuf.at[pl.ds(0, 8)], core1_s.at[0])
    taken(sib, core2_s.at[0])
    reduce1.finish(part1.at[pl.ds(0, 6)], zsend1)
    reduce2.finish(tbuf.at[pl.ds(0, 6), :, 0], zsend2)


def local(layer_input, ln_gain, w_query, w_keyval, w_output, kv_cache, lengths):
    any_space = pl.BlockSpec(memory_space=pl.ANY)
    dma = pltpu.SemaphoreType.DMA
    scratch = [
        pltpu.SMEM((8,), jnp.int32),
        pltpu.VMEM((FEATURES,), F32),
        pltpu.VMEM((ROWS, OUT), BF16),
        pltpu.VMEM((16, ROWS, FEATURES), BF16),
        pltpu.VMEM((PAIR, FEATURES), BF16),
        pltpu.VMEM((FEATURES, COLS), BF16),
        pltpu.VMEM((KV, FEATURES), BF16),
        pltpu.VMEM((COLS, OUT), BF16),
        pltpu.VMEM((8, CACHE, 2 * HS), BF16),
        pltpu.VMEM((8, 128), F32),
        pltpu.VMEM((8, 8, 128), F32),
        pltpu.VMEM((16, 8, 128), F32),
        pltpu.VMEM((8, 2, HALF, 128), BF16),
        pltpu.VMEM((2, 2, HALF, 128), BF16),
        pltpu.VMEM((2, 2, 2, HALF, 128), BF16),
        pltpu.VMEM((2, HALF, 128), BF16),
        pltpu.VMEM((2, HALF, 128), BF16),
        pltpu.VMEM((2, HALF, 128), F32),
        pltpu.VMEM((16, 16, 512), BF16),
        pltpu.VMEM((16, 16, 512), BF16),
        pltpu.VMEM((6, 128, 128), F32),
        pltpu.VMEM((8, 2 * HS), F32),
        pltpu.VMEM((8, HQ, CACHE), F32),
        pltpu.VMEM((6, 128, 128), F32),
        pltpu.VMEM((16, 16, 384), BF16),
        pltpu.VMEM((16, 16, 384), BF16),
        pltpu.VMEM((8, PAIR, COLS), BF16),
        pltpu.VMEM((8, 3, 2, ROWS, 768), BF16),
        pltpu.VMEM((8, 3, ROWS, 768), BF16),
        pltpu.VMEM((2, 2, 3, 32, 768), BF16),
        pltpu.VMEM((2, 2, 3, 2, 32, 768), BF16),
        pltpu.VMEM((3, 2, 32, 768), BF16),
        pltpu.VMEM((3, 2, 32, 768), BF16),
        pltpu.VMEM((3, 2, 32, 768), F32),
        dma((7,)), dma((3,)),
        dma((1,)), dma((1,)), dma((1,)), dma((16,)),
        dma((1,)), dma((12,)), dma((1,)), dma((8,)),
        dma((1,)), dma((2, 2, 3)), dma((2, 2, 3)), dma((1,)), dma((3,)),
        dma((1,)), dma((1,)), dma((1,)), dma((1,)),
        dma((1,)), dma((12,)), dma((1,)), dma((8, 3)),
        dma((1,)), dma((2, 2, 3)), dma((2, 2, 3)), dma((1,)), dma((3,)),
    ]
    return pl.pallas_call(
        kernel,
        name="decode_attention",
        out_shape=pltpu.VMEM((ROWS, OUT), BF16),
        in_specs=[any_space] * 7,
        out_specs=pl.BlockSpec(memory_space=pltpu.VMEM),
        scratch_shapes=scratch,
        compiler_params=pltpu.CompilerParams(
            collective_id=0, has_side_effects=True, vmem_limit_bytes=60 << 20
        ),
        cost_estimate=pl.CostEstimate(flops=8_300_000_000, bytes_accessed=25_000_000, transcendentals=800_000),
    )(lengths, ln_gain, layer_input, w_query, w_keyval.T, w_output, kv_cache)


def solution(mesh):
    in_specs = (
        P("gy", "gx"),
        P("gx"),
        P("gx", "gy"),
        P("gx", "gy"),
        P("gy", "gx"),
        P(("gx", "gy"), None, None),
        P(("gx", "gy")),
    )
    out_specs = P("gy", "gx")
    return jax.shard_map(local, mesh=mesh, in_specs=in_specs, out_specs=out_specs, check_vma=False)
```
